128 devices in a mesh: row: 8 (over x, core), col: 8 (over y, z_lo), rep: 2 (over z_hi).
Axes of the slice: x: 4, y: 4, z: 4 (z_hi: 2, z_lo: 2; z = z_hi * 2 + z_lo), core: 2. Of those that a mesh axis runs over, the one named last changes fastest.
Arguments:
- atom_feats: bfloat16 [2, 3072, 128], P('rep', ('row', 'col')), may hold values from -6 to 6
- atom_token: int32 [2, 3072], P('rep', ('row', 'col')), may hold values from 0 to 383, as said below
- atom_counts: int32 [2, 384], P('rep'), may hold values from 1 to 15, as said below
- restype: int32 [2, 384], P('rep'), may hold values from 0 to 31
- pair_in: bfloat16 [2, 384, 384, 128], P('rep', 'row', 'col'), may hold values from -6 to 6
- pair_mask: int32 [2, 384, 384], P('rep', 'row', 'col'), may hold values 0 or 1
- w_atom: bfloat16 [128, 384], replicated, may hold values from -0.5 to 0.5
- w_restype: bfloat16 [32, 384], replicated, may hold values from -6 to 6
- w_pair: bfloat16 [384, 256], replicated, may hold values from -0.3125 to 0.3125
- ln_tri: float32 [2, 128], replicated, may hold values from 0.5 to 1.5
- w_tri_in: bfloat16 [2, 128, 640], replicated, may hold values from -0.5 to 0.5
- ln_tri_out: float32 [2, 128], replicated, may hold values from 0.5 to 1.5
- w_tri_out: bfloat16 [2, 128, 128], replicated, may hold values from -0.5 to 0.5
- ln_trans: float32 [128], replicated, may hold values from 0.5 to 1.5
- w_up: bfloat16 [128, 1024], replicated, may hold values from -0.5 to 0.5
- w_down: bfloat16 [512, 128], replicated, may hold values from -0.25 to 0.25
- d_pair: bfloat16 [2, 384, 384, 128], P('rep', 'row', 'col'), may hold values from -0.03125 to 0.03125
Outputs:
- pair_out: bfloat16 [2, 384, 384, 128], P('rep', 'row', 'col')
- grad_down: float32 [512, 128], P(('row', 'col', 'rep'))
The draws below stay inside these ranges and needn't reach their ends.
Inputs may be any that keep to these rules, and one draw needn't show every extreme that they name: `atom_counts`: every token has 1 to 15 atoms and a complex's counts sum to 3072; the tokens fall into pairs whose counts sum to 16. Atoms are listed token after token: in each complex atom_token never falls and names token t on exactly atom_counts[t] atoms.
All inputs are finite; a program needn't handle non-finite values. No bound on the sum of `pair_mask` on one device may be relied on, other than what follows from the above.
Results may differ from the reference program's by a relative error of at most 0.027.
Values may be sent and summed in bfloat16 or wider, within the bound.
No kernel may reach another device: no remote copies, remote signals or barrier semaphores. Data moves between devices by JAX's collectives and lax.ppermute only.
A program may use at most 128 MiB of HBM per device.

```python
import jax
import jax.numpy as jnp
from jax import lax

C = 128
CH = 128
FH = 512
CA = 128
CS = 384
RESTYPES = 32
APT = 8
REPLICAS = 2
TOKENS = 384
ATOMS = 3072


def token_layout(key):

    def one_replica(replica_key):
        shuffle_key, value_key = jax.random.split(replica_key)
        shuffle = jax.random.permutation(shuffle_key, TOKENS)
        halves = jax.random.randint(value_key, (TOKENS // 2,), 1, 2 * APT)
        halves = halves.at[0].set(1)
        values = jnp.concatenate([halves, 2 * APT - halves]).astype(jnp.int32)
        counts = jnp.zeros((TOKENS,), jnp.int32).at[shuffle].set(values)
        boundaries = jnp.cumsum(counts)
        owners = jnp.searchsorted(boundaries, jnp.arange(ATOMS, dtype=jnp.int32), side='right').astype(jnp.int32)
        return (counts, owners)
    replica_keys = jax.random.split(key, REPLICAS)
    return jax.vmap(one_replica)(replica_keys)


def draw_atom_token(key, part):
    counts, owners = token_layout(key)
    return owners


def draw_atom_counts(key, part):
    counts, owners = token_layout(key)
    return counts


def place_ends(drawn, own_key, least, high):
    longest = drawn.shape.index(max(drawn.shape))
    spots = []
    for shift in (0, 1):
        where = [jax.random.randint(jax.random.fold_in(own_key, axis), (), 0, length) for axis, length in enumerate(drawn.shape)]
        where[longest] = (where[longest] + shift) % drawn.shape[longest]
        spots.append(tuple(where))
    return drawn.at[spots[0]].set(least).at[spots[1]].set(high)


def levels(key, shape, cuts, least, top_value):
    loudness, own = 1.0, jax.random.fold_in(key, 6)
    for position, shards_of in cuts:
        heights = jnp.exp(jax.random.uniform(jax.random.fold_in(own, position), (shards_of,), jnp.float32, least / len(cuts), top_value / len(cuts)))
        loudness = loudness * jnp.repeat(heights, shape[position] // shards_of).reshape([-1 if axis == position else 1 for axis in range(len(shape))])
    return loudness


def gaussian(stream_key, extent, deviation, reach, cuts=(), kind=jnp.bfloat16):
    entries = deviation * jax.random.normal(stream_key, extent, jnp.float32)
    if cuts:
        entries = entries * levels(stream_key, extent, cuts, -0.22, 0.18)
    return jnp.clip(entries, -reach, reach).astype(kind)


def setup_inputs(seed: int = 0) -> dict:
    splits = jax.random.split(jax.random.key(seed), 18)
    atom_feats = gaussian(splits[0], (REPLICAS, ATOMS, CA), 1.0, 6.0, ((0, 2), (1, 64)))
    atom_token = draw_atom_token(jax.random.fold_in(splits[17], 71), 0)
    atom_counts = draw_atom_counts(jax.random.fold_in(splits[17], 71), 0)
    restype = place_ends(jax.random.randint(splits[3], (REPLICAS, TOKENS), 0, RESTYPES), jax.random.fold_in(splits[3], 1), 0, RESTYPES - 1).astype(jnp.int32)
    pair_in = gaussian(splits[4], (REPLICAS, TOKENS, TOKENS, C), 1.0, 6.0, ((0, 2), (1, 8), (2, 8)))
    pair_mask = place_ends((jax.random.randint(splits[5], (REPLICAS, TOKENS, TOKENS), 0, 8) < 7).astype(jnp.int32), jax.random.fold_in(splits[5], 1), 0, 1)
    w_atom = gaussian(splits[6], (CA, CS), CA ** -0.5, 0.5)
    w_restype = gaussian(splits[7], (RESTYPES, CS), 1.0, 6.0)
    w_pair = gaussian(splits[8], (CS, 2 * C), CS ** -0.5, 0.3125)
    ln_tri = jnp.clip(jax.random.uniform(splits[9], (2, C), jnp.float32, 0.5, 1.5), 0.5, 1.5)
    w_tri_in = gaussian(splits[10], (2, C, 4 * CH + C), C ** -0.5, 0.5)
    ln_tri_out = jnp.clip(jax.random.uniform(splits[11], (2, CH), jnp.float32, 0.5, 1.5), 0.5, 1.5)
    w_tri_out = gaussian(splits[12], (2, CH, C), CH ** -0.5, 0.5)
    ln_trans = jnp.clip(jax.random.uniform(splits[13], (C,), jnp.float32, 0.5, 1.5), 0.5, 1.5)
    w_up = gaussian(splits[14], (C, 2 * FH), C ** -0.5, 0.5)
    w_down = gaussian(splits[15], (FH, C), FH ** -0.5, 0.25)
    d_pair = gaussian(splits[16], (REPLICAS, TOKENS, TOKENS, C), (2.0 / TOKENS), 0.03125, ((0, 2), (1, 8), (2, 8)))
    return dict(atom_feats=atom_feats, atom_token=atom_token, atom_counts=atom_counts, restype=restype, pair_in=pair_in, pair_mask=pair_mask, w_atom=w_atom, w_restype=w_restype, w_pair=w_pair, ln_tri=ln_tri, w_tri_in=w_tri_in, ln_tri_out=ln_tri_out, w_tri_out=w_tri_out, ln_trans=ln_trans, w_up=w_up, w_down=w_down, d_pair=d_pair)


def layer_norm(values, scales):
    average = lax.optimization_barrier(jnp.mean(values, axis=-1, keepdims=True))
    centred = values - average
    variance = lax.optimization_barrier(jnp.mean(centred * centred, axis=-1, keepdims=True))
    return centred * lax.rsqrt(variance + 1e-05) * scales

def project(pair_block, scales, weights, validity, inner):
    normed = layer_norm(pair_block.astype(jnp.float32), scales).astype(jnp.bfloat16)
    projected = jnp.dot(normed, weights, preferred_element_type=jnp.float32)
    first_side = (jax.nn.sigmoid(projected[..., :inner]) * projected[..., inner:2 * inner] * validity).astype(jnp.bfloat16)
    second_side = (jax.nn.sigmoid(projected[..., 2 * inner:3 * inner]) * projected[..., 3 * inner:4 * inner] * validity).astype(jnp.bfloat16)
    gating = jax.nn.sigmoid(projected[..., 4 * inner:])
    return (first_side, second_side, gating)

def finish(pair_block, triangle, scales, weights, gating):
    normed = layer_norm(triangle, scales).astype(jnp.bfloat16)
    update = jnp.dot(normed, weights, preferred_element_type=jnp.float32)
    return (pair_block.astype(jnp.float32) + gating * update).astype(jnp.bfloat16)

def reference(atom_feats, atom_token, atom_counts, restype, pair_in, pair_mask, w_atom, w_restype, w_pair, ln_tri, w_tri_in, ln_tri_out, w_tri_out, ln_trans, w_up, w_down, d_pair):
    outputs = []
    grad_total = jnp.zeros((FH, C), jnp.float32)
    for replica in range(REPLICAS):
        activated = jax.nn.relu(jnp.dot(atom_feats[replica], w_atom, preferred_element_type=jnp.float32)).astype(jnp.bfloat16)
        token_sums = jax.ops.segment_sum(activated.astype(jnp.float32), atom_token[replica], num_segments=TOKENS)
        embedded = w_restype[restype[replica]].astype(jnp.float32)
        single = (token_sums / atom_counts[replica].astype(jnp.float32)[:, None] + embedded).astype(jnp.bfloat16)
        sides = jnp.dot(single, w_pair, preferred_element_type=jnp.float32).astype(jnp.bfloat16)
        left_rows = sides[:, :C].astype(jnp.float32)
        right_rows = sides[:, C:].astype(jnp.float32)
        pair_block = (pair_in[replica].astype(jnp.float32) + left_rows[:, None, :] + right_rows[None, :, :]).astype(jnp.bfloat16)
        validity = pair_mask[replica].astype(jnp.float32)[..., None]
        first_side, second_side, gating = project(pair_block, ln_tri[0], w_tri_in[0], validity, CH)
        triangle = jnp.einsum('ikc,jkc->ijc', first_side.astype(jnp.float32), second_side.astype(jnp.float32))
        pair_block = finish(pair_block, triangle, ln_tri_out[0], w_tri_out[0], gating)
        first_side, second_side, gating = project(pair_block, ln_tri[1], w_tri_in[1], validity, CH)
        triangle = jnp.einsum('kic,kjc->ijc', first_side.astype(jnp.float32), second_side.astype(jnp.float32))
        pair_block = finish(pair_block, triangle, ln_tri_out[1], w_tri_out[1], gating)
        normed = layer_norm(pair_block.astype(jnp.float32), ln_trans).astype(jnp.bfloat16)
        expanded = jnp.dot(normed, w_up, preferred_element_type=jnp.float32)
        hidden = (jax.nn.silu(expanded[..., :FH]) * expanded[..., FH:]).astype(jnp.bfloat16)
        result = (pair_block.astype(jnp.float32) + jnp.dot(hidden, w_down, preferred_element_type=jnp.float32)).astype(jnp.bfloat16)
        outputs.append(result)
        flat_hidden = hidden.reshape(TOKENS * TOKENS, FH)
        flat_grad = d_pair[replica].reshape(TOKENS * TOKENS, C)
        grad_total = grad_total + jnp.dot(flat_hidden.T, flat_grad, preferred_element_type=jnp.float32)
    return (jnp.stack(outputs, axis=0), grad_total)
```

```python
import jax
import jax.numpy as jnp
from jax import lax
from jax.sharding import PartitionSpec as P

GRID = ("row", "col")


def layer_norm(values, scales, axis):
    average = jnp.mean(values, axis=axis, keepdims=True)
    centred = values - average
    variance = jnp.mean(centred * centred, axis=axis, keepdims=True)
    return centred * lax.rsqrt(variance + 1e-05) * scales


def exchange(value, axes):
    return lax.all_to_all(value, axes, 0, 0, tiled=True)


def local(
    atom_feats,
    atom_token,
    atom_counts,
    restype,
    pair_in,
    pair_mask,
    w_atom,
    w_restype,
    w_pair,
    ln_tri,
    w_tri_in,
    ln_tri_out,
    w_tri_out,
    ln_trans,
    w_up,
    w_down,
    d_pair,
):
    rows, cols = lax.axis_size("row"), lax.axis_size("col")
    devices = rows * cols
    tok_dev = pair_in.shape[1]
    width = pair_in.shape[3]
    inner = w_tri_out.shape[1]
    expand = w_down.shape[0]
    tokens_all = atom_counts.shape[1]
    share = inner // devices
    row_index = lax.axis_index("row")
    col_index = lax.axis_index("col")
    counts_all = atom_counts[0]

    feats = exchange(jnp.broadcast_to(atom_feats, (devices,) + atom_feats.shape[1:]), GRID)
    feats = feats.reshape(-1, feats.shape[-1])
    activated = jax.nn.relu(jnp.dot(feats, w_atom, preferred_element_type=jnp.float32)).astype(
        jnp.bfloat16
    )
    ends = jnp.cumsum(counts_all)
    starts = ends - counts_all

    def pick(start, w_columns):
        def cut(values):
            return lax.dynamic_slice_in_dim(values, start, tok_dev, 0)

        atoms = jnp.arange(feats.shape[0], dtype=jnp.int32)
        owners = (
            (atoms[None, :] >= cut(starts)[:, None]) & (atoms[None, :] < cut(ends)[:, None])
        ).astype(jnp.bfloat16)
        sums = jnp.dot(owners, activated, preferred_element_type=jnp.float32)
        kinds = jnp.arange(w_restype.shape[0], dtype=jnp.int32)
        picked = (cut(restype[0])[:, None] == kinds[None, :]).astype(jnp.bfloat16)
        embedded = jnp.dot(picked, w_restype, preferred_element_type=jnp.float32)
        single = (sums / cut(counts_all).astype(jnp.float32)[:, None] + embedded).astype(
            jnp.bfloat16
        )
        return jnp.dot(single, w_columns, preferred_element_type=jnp.float32).astype(jnp.bfloat16)

    left_rows = pick(row_index * tok_dev, w_pair[:, :width])
    right_rows = pick(col_index * tok_dev, w_pair[:, width:])
    pair_block = (
        pair_in[0].astype(jnp.float32)
        + left_rows.astype(jnp.float32)[:, None, :]
        + right_rows.astype(jnp.float32)[None, :, :]
    ).astype(jnp.bfloat16)
    validity = pair_mask[0].astype(jnp.float32)[..., None]

    for update in range(2):
        normed = layer_norm(pair_block.astype(jnp.float32), ln_tri[update], -1).astype(jnp.bfloat16)
        proj = jnp.dot(normed, w_tri_in[update], preferred_element_type=jnp.float32)
        parts = [proj[..., n * inner : (n + 1) * inner] for n in range(4)]
        gating = jax.nn.sigmoid(proj[..., 4 * inner :])
        first = (jax.nn.sigmoid(parts[0]) * parts[1] * validity).astype(jnp.bfloat16)
        second = (jax.nn.sigmoid(parts[2]) * parts[3] * validity).astype(jnp.bfloat16)
        both = jnp.stack([first, second], 0).reshape(2, tok_dev * tok_dev, devices, share)
        both = exchange(
            both.transpose(2, 0, 3, 1).reshape(devices, 2 * share, tok_dev * tok_dev), GRID
        )
        both = both.reshape(rows, cols, 2, share, tok_dev, tok_dev).transpose(2, 3, 0, 4, 1, 5)
        both = both.reshape(2, share, tokens_all, tokens_all)
        form = "cik,cjk->cij" if update == 0 else "cki,ckj->cij"
        triangle = jnp.einsum(form, both[0], both[1], preferred_element_type=jnp.float32)
        triangle = triangle.astype(jnp.bfloat16).reshape(share, rows, tok_dev, cols, tok_dev)
        triangle = triangle.transpose(1, 3, 0, 2, 4).reshape(devices, share, tok_dev * tok_dev)
        triangle = exchange(triangle, GRID).reshape(inner, tok_dev * tok_dev).astype(jnp.float32)
        t_normed = layer_norm(triangle, ln_tri_out[update][:, None], 0).astype(jnp.bfloat16)
        change = lax.dot_general(
            t_normed,
            w_tri_out[update],
            (((0,), (0,)), ((), ())),
            preferred_element_type=jnp.float32,
        ).reshape(tok_dev, tok_dev, width)
        pair_block = (pair_block.astype(jnp.float32) + gating * change).astype(jnp.bfloat16)

    normed = layer_norm(pair_block.astype(jnp.float32), ln_trans, -1).astype(jnp.bfloat16)
    expanded = jnp.dot(normed, w_up, preferred_element_type=jnp.float32)
    hidden = (jax.nn.silu(expanded[..., :expand]) * expanded[..., expand:]).astype(jnp.bfloat16)
    pair_result = (
        pair_block.astype(jnp.float32) + jnp.dot(hidden, w_down, preferred_element_type=jnp.float32)
    ).astype(jnp.bfloat16)
    flat_hidden = hidden.reshape(tok_dev * tok_dev, expand)
    flat_grad = d_pair[0].reshape(tok_dev * tok_dev, width)
    grad = jnp.einsum("ef,ec->fc", flat_hidden, flat_grad, preferred_element_type=jnp.float32)
    everyone = devices * lax.axis_size("rep")
    grad = exchange(grad.reshape(everyone, expand // everyone, width), ("row", "col", "rep"))
    return (pair_result[None], jnp.sum(grad, axis=0))


def solution(mesh):
    return jax.shard_map(
        local,
        mesh=mesh,
        in_specs=(
            P("rep", ("row", "col"), None),
            P("rep", ("row", "col")),
            P("rep", None),
            P("rep", None),
            P("rep", "row", "col", None),
            P("rep", "row", "col"),
            P(),
            P(),
            P(),
            P(),
            P(),
            P(),
            P(),
            P(),
            P(),
            P(),
            P("rep", "row", "col", None),
        ),
        out_specs=(P("rep", "row", "col", None), P(("row", "col", "rep"), None)),
        check_vma=False,
    )
```

```python
import functools

import jax
import jax.numpy as jnp
from jax import lax
from jax.experimental import pallas as pl
from jax.experimental.pallas import tpu as pltpu
from jax.sharding import PartitionSpec as P

F32, BF16 = jnp.float32, jnp.bfloat16
LANES = 128
PARAMS = pltpu.CompilerParams(vmem_limit_bytes=40 * 2**20)


def nt(a, b):
    return lax.dot_general(a, b, (((1,), (1,)), ((), ())), preferred_element_type=F32)


def nn(a, b):
    return lax.dot_general(a, b, (((1,), (0,)), ((), ())), preferred_element_type=F32)


def tn(a, b):
    return lax.dot_general(a, b, (((0,), (0,)), ((), ())), preferred_element_type=F32)


def norm(values, scales, axis):
    average = jnp.mean(values, axis=axis, keepdims=True)
    centred = values - average
    variance = jnp.mean(centred * centred, axis=axis, keepdims=True)
    return centred * lax.rsqrt(variance + 1e-05) * scales


def sigmoid(x):
    return jax.nn.sigmoid(x)


def exchange(value, axes):
    return lax.all_to_all(value, axes, 0, 0, tiled=True)


def send_group(g, normed, weights, mask_row, wide, devices):
    proj = nt(weights, normed)
    half = proj.shape[0] // 2
    sides = sigmoid(proj[:half]) * proj[half:] * mask_row
    rows = wide.shape[0] // devices
    parts = sides.shape[1] // LANES
    kinds = half // devices
    for kind in range(kinds):
        for q in range(parts):
            wide[pl.ds((g * kinds + kind) * parts + q, devices, stride=rows), :] = sides[
                kind * devices : (kind + 1) * devices, q * LANES : (q + 1) * LANES
            ]


def front_kernel(feats, tokens, w_atom, w_restype, w_pair, pair_in, mask, gain, weights, send, sides, wide):
    tok = pair_in.shape[0]
    width = pair_in.shape[2]
    devices = send.shape[0]
    starts, ends = tokens[:, 0:1], tokens[:, 1:2]
    counts, types = tokens[:, 2:3], tokens[:, 3:4]
    chunk = 512

    def pool(n, sums):
        at = pl.multiple_of(n * chunk, chunk)
        act = jnp.maximum(nn(feats[pl.ds(at, chunk), :], w_atom[...]), 0.0).astype(BF16)
        atoms = lax.broadcasted_iota(jnp.int32, (2 * tok, chunk), 1) + at
        owners = jnp.where((atoms >= starts) & (atoms < ends), 1.0, 0.0).astype(BF16)
        return sums + nn(owners, act)

    sums = lax.fori_loop(
        0, feats.shape[0] // chunk, pool, jnp.zeros((2 * tok, w_atom.shape[1]), F32)
    )
    kinds = lax.broadcasted_iota(jnp.int32, (2 * tok, w_restype.shape[0]), 1)
    embedded = nn(jnp.where(kinds == types, 1.0, 0.0).astype(BF16), w_restype[...])
    single = (sums / counts.astype(F32) + embedded).astype(BF16)
    sides[:tok, :] = nn(single[:tok], w_pair[:, :width]).astype(BF16)
    sides[tok:, :] = nn(single[tok:], w_pair[:, width:]).astype(BF16)
    right = sides[tok:, :].astype(F32)

    def group(g, carry):
        at = pl.multiple_of(g * 8, 8)
        left = sides[pl.ds(at, 8), :].astype(F32)
        block = pair_in[pl.ds(at, 8)].astype(F32) + left[:, None, :] + right[None]
        block = block.astype(BF16).astype(F32).reshape(8 * tok, width)
        normed = norm(block, gain[...], -1).astype(BF16)
        send_group(g, normed, weights[...], mask[pl.ds(g, 1), :], wide, devices)
        return carry

    lax.fori_loop(0, tok // 8, group, 0)
    send[...] = wide[...].astype(BF16).reshape(send.shape)


def first_gate_kernel(pair_in, sides, gain, w_gate, pair, gate):
    tok = pair_in.shape[0]
    width = pair_in.shape[2]
    left = sides[:tok, :].astype(F32)

    def group(g, carry):
        at = pl.multiple_of(g * 8, 8)
        right = sides[pl.ds(tok + at, 8), :].astype(F32)
        block = pair_in[pl.ds(at, 8)].astype(F32) + left[None] + right[:, None, :]
        block = block.astype(BF16).reshape(8 * tok, width)
        rows = pl.ds(pl.multiple_of(g * 8 * tok, 8 * tok), 8 * tok)
        pair[rows, :] = block
        normed = norm(block.astype(F32), gain[...], -1).astype(BF16)
        gate[rows, :] = sigmoid(nn(normed, w_gate[...]))
        return carry

    lax.fori_loop(0, tok // 8, group, 0)


def gate_kernel(pair, gain, w_gate, gate):
    span = 384

    def group(g, carry):
        rows = pl.ds(pl.multiple_of(g * span, span), span)
        normed = norm(pair[rows, :].astype(F32), gain[...], -1).astype(BF16)
        gate[rows, :] = sigmoid(nn(normed, w_gate[...]))
        return carry

    lax.fori_loop(0, pair.shape[0] // span, group, 0)


def windows_of(parts, tok):
    lane = lax.broadcasted_iota(jnp.int32, parts[0].shape, 1)
    out = []
    for w in range(len(parts) * LANES // tok):
        q, off = divmod(w * tok, LANES)
        value = parts[q] if off == 0 else pltpu.roll(parts[q], LANES - off, 1)
        if off + tok > LANES:
            value = jnp.where(lane < LANES - off, value, pltpu.roll(parts[q + 1], LANES - off, 1))
        out.append(value)
    return out


def triangle_kernel(tok, blocks, x, out, xf, lhs, rhs, moved, of):
    devices = x.shape[0]
    share = out.shape[1] * LANES // (tok * tok)
    parts = 3
    groups = tok // 8
    kinds = 2 * share
    side_len = blocks * tok
    xf[...] = x[...].astype(F32).reshape(xf.shape)
    lane = lax.broadcasted_iota(jnp.int32, (tok, LANES), 1)
    per_block = devices // blocks * x.shape[1]

    def unpack(b, carry):
        cols = pl.ds(pl.multiple_of(b * LANES, LANES), LANES)
        for kind in range(kinds):
            side, e = divmod(kind, share)
            tiles = [
                xf[pl.ds(b * per_block + kind * parts + q, tok, stride=kinds * parts), :]
                for q in range(parts)
            ]
            for w, value in enumerate(windows_of(tiles, tok)):
                if side == 0:
                    rhs[e, w * tok : (w + 1) * tok, cols] = jnp.where(lane < tok, value, 0.0).astype(BF16)
                else:
                    lhs[e, w * tok : (w + 1) * tok, cols] = value.astype(BF16)
        return carry

    lax.fori_loop(0, blocks, unpack, 0)

    source = lax.broadcasted_iota(jnp.int32, (side_len, blocks * LANES), 0)
    target = lax.broadcasted_iota(jnp.int32, (side_len, blocks * LANES), 1)
    block, spot = target // LANES, target % LANES
    wanted = (spot % 8) * tok + block * groups + spot // 8
    place = jnp.where((source == wanted) & (spot < tok), 1.0, 0.0).astype(BF16)
    for e in range(share):
        product = nt(lhs[e], rhs[e]).astype(BF16)
        moved[e] = nn(product, place)

    def pack(b, carry):
        cols = pl.ds(pl.multiple_of(b * LANES, LANES), LANES)
        for e in range(share):
            tiles = [None] * parts
            for w in range(8):
                value = moved[e, w * tok : (w + 1) * tok, cols]
                q, off = divmod(w * tok, LANES)
                first = value if off == 0 else pltpu.roll(value, off, 1)
                tiles[q] = first if tiles[q] is None else jnp.where(lane >= off, first, tiles[q])
                if off + tok > LANES:
                    tiles[q + 1] = first
            for q in range(parts):
                at = b * blocks * out.shape[1] + e * parts + q
                of[pl.ds(at, tok, stride=share * parts), :] = tiles[q]
        return carry

    lax.fori_loop(0, blocks, pack, 0)
    out[...] = of[...].astype(BF16).reshape(out.shape)


def updated_group(g, tri, wide, gain, w_out, pair, gate, rows):
    devices, each = tri.shape[0], tri.shape[1]
    parts = 3
    share = w_out.shape[0] // devices
    changes = []
    for q in range(parts):
        tile = jnp.concatenate(
            [
                wide[pl.ds(g * share * parts + e * parts + q, devices, stride=each), :]
                for e in range(share)
            ],
            axis=0,
        )
        normed = norm(tile, gain[...], 0).astype(BF16)
        changes.append(tn(normed, w_out[...]))
    change = jnp.concatenate(changes, axis=0)
    return (pair[rows, :].astype(F32) + gate[rows, :] * change).astype(BF16)


def middle_kernel(tri, pair, gate, gain_out, w_out, mask, gain, weights, send, pair_new, thin, wide):
    devices = tri.shape[0]
    thin[...] = tri[...].astype(F32).reshape(thin.shape)
    span = 384

    def group(g, carry):
        rows = pl.ds(pl.multiple_of(g * span, span), span)
        block = updated_group(g, tri, thin, gain_out, w_out, pair, gate, rows)
        pair_new[rows, :] = block
        normed = norm(block.astype(F32), gain[...], -1).astype(BF16)
        send_group(g, normed, weights[...], mask[pl.ds(g, 1), :], wide, devices)
        return carry

    lax.fori_loop(0, pair.shape[0] // span, group, 0)
    send[...] = wide[...].astype(BF16).reshape(send.shape)


def last_kernel(tri, pair, gate, gain_out, w_out, gain, w_up, d_pair, grad, hidden, pair_new, thin, total):
    thin[...] = tri[...].astype(F32).reshape(thin.shape)
    total[...] = jnp.zeros_like(total)
    span = 384
    expand = total.shape[0]

    def group(g, carry):
        rows = pl.ds(pl.multiple_of(g * span, span), span)
        block = updated_group(g, tri, thin, gain_out, w_out, pair, gate, rows)
        pair_new[rows, :] = block
        normed = norm(block.astype(F32), gain[...], -1).astype(BF16)
        up = nt(w_up[...], normed)
        first = up[:expand]
        units = (first * sigmoid(first) * up[expand:]).astype(BF16)
        hidden[g] = units
        total[...] += nn(units, d_pair[rows, :])
        return carry

    lax.fori_loop(0, pair.shape[0] // span, group, 0)
    grad[...] = total[...]


def down_kernel(hidden, pair, w_down, out, wide):
    tok = out.shape[0]
    span = hidden.shape[2]
    each = span // tok

    def group(g, carry):
        rows = pl.ds(pl.multiple_of(g * span, span), span)
        result = pair[rows, :].astype(F32) + tn(hidden[g], w_down[...])
        for n in range(each):
            wide[pl.ds(g * each + n, tok, stride=tok), :] = result[n * tok : (n + 1) * tok]
        return carry

    lax.fori_loop(0, hidden.shape[0], group, 0)
    out[...] = wide[...].astype(BF16).reshape(out.shape)


def call(kernel, outs, scratch, name, cost, *args):
    return pl.pallas_call(
        kernel,
        out_shape=outs,
        in_specs=[pl.BlockSpec(memory_space=pltpu.VMEM)] * len(args),
        out_specs=jax.tree.map(lambda _: pl.BlockSpec(memory_space=pltpu.VMEM), outs),
        scratch_shapes=scratch,
        compiler_params=PARAMS,
        name=name,
        cost_estimate=pl.CostEstimate(flops=cost, bytes_accessed=4 * 2**20, transcendentals=10**6),
    )(*args)


def local(
    atom_feats,
    atom_token,
    atom_counts,
    restype,
    pair_in,
    pair_mask,
    w_atom,
    w_restype,
    w_pair,
    ln_tri,
    w_tri_in,
    ln_tri_out,
    w_tri_out,
    ln_trans,
    w_up,
    w_down,
    d_pair,
):
    n_row, n_col = lax.axis_size("row"), lax.axis_size("col")
    devices = n_row * n_col
    tok = pair_in.shape[1]
    width = pair_in.shape[3]
    inner = w_tri_out.shape[1]
    expand = w_down.shape[0]
    share = inner // devices
    count = tok * tok
    groups = tok // 8
    span = 8 * tok
    row_start = lax.axis_index("row") * tok
    col_start = lax.axis_index("col") * tok

    feats = exchange(jnp.broadcast_to(atom_feats, (devices,) + atom_feats.shape[1:]), ("row", "col"))
    feats = feats.reshape(-1, feats.shape[-1])

    ends = jnp.cumsum(atom_counts[0])
    table = jnp.stack([ends - atom_counts[0], ends, atom_counts[0], restype[0]], axis=1)
    tokens = jnp.concatenate(
        [lax.dynamic_slice_in_dim(table, start, tok, 0) for start in (row_start, col_start)], 0
    )
    valid = pair_mask[0].astype(F32)
    masks = [valid.reshape(groups, span), valid.T.reshape(groups, span)]
    turned_in = pair_in[0].transpose(1, 0, 2)
    turned_grad = d_pair[0].transpose(1, 0, 2).reshape(count, width)
    w_sides = (
        w_tri_in[:, :, : 4 * inner]
        .reshape(2, width, 2, 2, devices, share)
        .transpose(0, 3, 2, 5, 4, 1)
        .reshape(2, 4 * inner, width)
    )
    w_gates = w_tri_in[:, :, 4 * inner :]
    w_up_turned = w_up.T

    def by_owner(values, update):
        if update == 0:
            order = values.reshape((n_col, n_row, share) + values.shape[1:]).swapaxes(0, 1)
        else:
            order = values.reshape((n_row, n_col, share) + values.shape[1:])
        return jnp.moveaxis(order, 2, 0).reshape(values.shape)

    w_outs = [by_owner(w_tri_out[u], u) for u in range(2)]
    gains_out = [by_owner(ln_tri_out[u][:, None], u) for u in range(2)]
    gains = [ln_tri[0:1], ln_tri[1:2], ln_trans[None]]

    shape = jax.ShapeDtypeStruct
    rows_out = 2 * share * count // LANES
    rows_back = share * count // LANES
    send_shape = shape((devices, rows_out, LANES), BF16)
    back_shape = shape((devices, rows_back, LANES), BF16)
    wide = pltpu.VMEM((devices * rows_out, LANES), F32)
    thin = pltpu.VMEM((devices * rows_back, LANES), F32)
    flat = shape((count, width), BF16)
    flat_wide = shape((count, width), F32)
    cost = 400 * 10**6

    def triangle(value):
        blocks = n_row
        return call(
            functools.partial(triangle_kernel, tok, blocks),
            back_shape,
            [
                wide,
                pltpu.VMEM((share, blocks * tok, blocks * LANES), BF16),
                pltpu.VMEM((share, blocks * tok, blocks * LANES), BF16),
                pltpu.VMEM((share, blocks * tok, blocks * LANES), F32),
                thin,
            ],
            "triangle",
            cost,
            value,
        )

    send, sides = call(
        front_kernel,
        (send_shape, shape((2 * tok, width), BF16)),
        [wide],
        "front",
        cost,
        feats,
        tokens,
        w_atom,
        w_restype,
        w_pair,
        pair_in[0],
        masks[0],
        gains[0],
        w_sides[0],
    )
    arrived = exchange(send, ("col", "row"))
    pair, gate = call(
        first_gate_kernel,
        (flat, flat_wide),
        [],
        "first_gate",
        cost,
        turned_in,
        sides,
        gains[0],
        w_gates[0],
    )
    tri = exchange(triangle(arrived), ("row", "col"))
    send, pair = call(
        middle_kernel,
        (send_shape, flat),
        [thin, wide],
        "middle",
        cost,
        tri,
        pair,
        gate,
        gains_out[0],
        w_outs[0],
        masks[1],
        gains[1],
        w_sides[1],
    )
    arrived = exchange(send, ("row", "col"))
    gate = call(gate_kernel, flat_wide, [], "gate", cost, pair, gains[1], w_gates[1])
    tri = exchange(triangle(arrived), ("row", "col"))
    grad, hidden, pair = call(
        last_kernel,
        (shape((expand, width), F32), shape((groups, expand, span), BF16), flat),
        [thin, pltpu.VMEM((expand, width), F32)],
        "last",
        2 * cost,
        tri,
        pair,
        gate,
        gains_out[1],
        w_outs[1],
        gains[2],
        w_up_turned,
        turned_grad,
    )
    everyone = devices * lax.axis_size("rep")
    grad = exchange(grad.reshape(everyone, expand // everyone, width), ("row", "col", "rep"))
    result = call(
        down_kernel,
        shape((tok, tok, width), BF16),
        [pltpu.VMEM((count, width), F32)],
        "down",
        cost,
        hidden,
        pair,
        w_down,
    )
    return (result[None], jnp.sum(grad, axis=0))


def solution(mesh):
    return jax.shard_map(
        local,
        mesh=mesh,
        in_specs=(
            P("rep", ("row", "col"), None),
            P("rep", ("row", "col")),
            P("rep", None),
            P("rep", None),
            P("rep", "row", "col", None),
            P("rep", "row", "col"),
            P(),
            P(),
            P(),
            P(),
            P(),
            P(),
            P(),
            P(),
            P(),
            P(),
            P("rep", "row", "col", None),
        ),
        out_specs=(P("rep", "row", "col", None), P(("row", "col", "rep"), None)),
        check_vma=False,
    )
```

```python
import functools

import jax
import jax.numpy as jnp
from jax import lax
from jax.experimental import pallas as pl
from jax.experimental.pallas import tpu as pltpu
from jax.sharding import PartitionSpec as P

F32, BF16 = jnp.float32, jnp.bfloat16
LANES = 128
UNROLL = 6
PARAMS = pltpu.CompilerParams(vmem_limit_bytes=20 * 2**20)


def nt(a, b):
    return lax.dot_general(a, b, (((1,), (1,)), ((), ())), preferred_element_type=F32)


def nn(a, b):
    return lax.dot_general(a, b, (((1,), (0,)), ((), ())), preferred_element_type=F32)


def norm(values, scales, axis):
    average = jnp.mean(values, axis=axis, keepdims=True)
    centred = values - average
    variance = jnp.mean(centred * centred, axis=axis, keepdims=True)
    return centred * lax.rsqrt(variance + 1e-05) * scales


def sigmoid(x):
    return jax.nn.sigmoid(x)


def exchange(value, axes):
    return lax.all_to_all(value, axes, 0, 0, tiled=True)


def send_group(g, normed, weights, mask_row, wide, devices):
    proj = nn(weights, normed)
    half = proj.shape[0] // 2
    sides = sigmoid(proj[:half]) * proj[half:] * mask_row
    rows = wide.shape[0] // devices
    parts = sides.shape[1] // LANES
    kinds = half // devices
    for kind in range(kinds):
        for q in range(parts):
            wide[pl.ds((g * kinds + kind) * parts + q, devices, stride=rows), :] = sides[
                kind * devices : (kind + 1) * devices, q * LANES : (q + 1) * LANES
            ]


def spread_kernel(value, out, copies, sems):
    several = copies.shape[0]
    copies[...] = jnp.broadcast_to(value[...], copies.shape)
    moves = [
        pltpu.make_async_copy(copies, out.at[pl.ds(n * several, several)], sems.at[n])
        for n in range(out.shape[0] // several)
    ]
    for move in moves:
        move.start()
    for move in moves:
        move.wait()


def prepare_kernel(place, pair_in, counts, types, plain, tokens, bounds, wide, made, sem):
    tok, width = pair_in.shape[0], pair_in.shape[2]
    span = 8 * tok
    wide[...] = pair_in[...].astype(F32).reshape(wide.shape)

    def turn(g, carry):
        rows = pl.ds(pl.multiple_of(g * span, span), span)
        made[g] = wide[rows, :].T.astype(BF16)
        return carry

    lax.fori_loop(0, tok // 8, turn, 0)
    move = pltpu.make_async_copy(made, plain, sem)
    move.start()
    shape = (2 * tok, counts.shape[1])
    slot = lax.broadcasted_iota(jnp.int32, shape, 0)
    mine = jnp.where(slot < tok, place[0] * tok + slot, place[1] * tok + slot - tok)
    token = lax.broadcasted_iota(jnp.int32, shape, 1)
    numbers = jnp.broadcast_to(counts[...].astype(F32), shape)
    kinds = jnp.broadcast_to(types[...].astype(F32), shape)

    def total(wanted, values):
        return jnp.sum(jnp.where(wanted, values, 0.0), axis=1, keepdims=True)

    columns = [
        total(token < mine, numbers),
        total(token <= mine, numbers),
        total(token == mine, numbers),
        total(token == mine, kinds),
    ]
    lane = lax.broadcasted_iota(jnp.int32, tokens.shape, 1)
    table = jnp.zeros(tokens.shape, F32)
    for n, column in enumerate(columns):
        table = jnp.where(lane == n, column, table)
    tokens[...] = table.astype(jnp.int32)
    every = lax.broadcasted_iota(jnp.int32, counts.shape, 1)
    for k in range(2):
        first = place[k] * tok
        start = jnp.sum(jnp.where(every < first, counts[...], 0))
        bounds[2 * k] = start // 16 * 16
        bounds[2 * k + 1] = jnp.sum(jnp.where(every < first + tok, counts[...], 0))
    move.wait()


def turned_rows(g, source, tok):
    rows = [source[pl.ds(g * 8 + n, tok, stride=tok), :] for n in range(8)]
    return jnp.concatenate(rows, axis=0)


def turn_kernel(d_pair, out, wide, made, sem):
    tok = d_pair.shape[0]
    span = 8 * tok
    wide[...] = d_pair[...].astype(F32).reshape(wide.shape)

    def grads(g, carry):
        rows = pl.ds(pl.multiple_of(g * span, span), span)
        made[rows, :] = turned_rows(g, wide, tok).astype(BF16)
        return carry

    lax.fori_loop(0, tok // 8, grads, 0)
    move = pltpu.make_async_copy(made, out, sem)
    move.start()
    move.wait()


def added_sides(g, sides, tok, turned):
    shape = (2 * tok, 8 * tok)
    source = lax.broadcasted_iota(jnp.int32, shape, 0)
    token = lax.broadcasted_iota(jnp.int32, shape, 1)
    high, low = g * 8 + token // tok, token % tok
    left, right = (low, high) if turned else (high, low)
    wanted = (source == left) | (source == right + tok)
    return nn(sides, jnp.where(wanted, 1.0, 0.0).astype(BF16))


def front_kernel(bounds, feats, tokens, w_atom, w_restype, w_pair, plain, mask, gain, weights, send, sides, wide, pair_in, sem):
    groups, width, span = plain.shape
    tok = span // 8
    devices = send.shape[0]
    move = pltpu.make_async_copy(plain, pair_in, sem)
    move.start()
    chunk = 384
    last = feats.shape[0] - chunk

    def pool(n, sums):
        out = []
        for k in range(2):
            base = bounds[2 * k] + n * chunk
            at = pl.multiple_of(jnp.minimum(base, last), 16)
            act = jnp.maximum(nn(feats[pl.ds(at, chunk), :], w_atom[...]), 0.0).astype(BF16)
            atoms = lax.broadcasted_iota(jnp.int32, (tok, chunk), 1) + at
            starts = tokens[k * tok : (k + 1) * tok, 0:1]
            ends = tokens[k * tok : (k + 1) * tok, 1:2]
            mine = (atoms >= jnp.maximum(starts, base)) & (atoms < ends)
            out.append(sums[k] + nn(jnp.where(mine, 1.0, 0.0).astype(BF16), act))
        return tuple(out)

    steps = jnp.maximum(bounds[1] - bounds[0], bounds[3] - bounds[2])
    zero = jnp.zeros((tok, w_atom.shape[1]), F32)
    sums = lax.fori_loop(0, (steps + chunk - 1) // chunk, pool, (zero, zero))
    counts, types = tokens[:, 2:3], tokens[:, 3:4]
    kinds = lax.broadcasted_iota(jnp.int32, (2 * tok, w_restype.shape[0]), 1)
    embedded = nn(jnp.where(kinds == types, 1.0, 0.0).astype(BF16), w_restype[...])
    single = (jnp.concatenate(sums, 0) / counts.astype(F32) + embedded).astype(BF16)
    left = nn(single[:tok], w_pair[:, :width])
    right = nn(single[tok:], w_pair[:, width:])
    sides[...] = jnp.concatenate([left, right], 0).T.astype(BF16)
    move.wait()

    def group(g, carry):
        block = pair_in[g].astype(F32) + added_sides(g, sides[...], tok, False)
        normed = norm(block.astype(BF16).astype(F32), gain[...], 0).astype(BF16)
        send_group(g, normed, weights[...], mask[pl.ds(g, 1), :], wide, devices)
        return carry

    lax.fori_loop(0, groups, group, 0, unroll=UNROLL)
    send[...] = wide[...].astype(BF16).reshape(send.shape)


def first_gate_kernel(pair_in, sides, gain, w_gate, pair_out, gate_out, wide, pair, gate, sems):
    tok = pair_in.shape[0]
    wide[...] = pair_in[...].astype(F32).reshape(wide.shape)

    def group(g, carry):
        block = turned_rows(g, wide, tok).T + added_sides(g, sides[...], tok, True)
        block = block.astype(BF16)
        pair[g] = block
        normed = norm(block.astype(F32), gain[...], 0).astype(BF16)
        gate[g] = sigmoid(nn(w_gate[...], normed))
        return carry

    lax.fori_loop(0, tok // 8, group, 0)
    moves = [
        pltpu.make_async_copy(pair, pair_out, sems.at[0]),
        pltpu.make_async_copy(gate, gate_out, sems.at[1]),
    ]
    for move in moves:
        move.start()
    for move in moves:
        move.wait()


def windows_of(parts, tok):
    lane = lax.broadcasted_iota(jnp.int32, parts[0].shape, 1)
    out = []
    for w in range(len(parts) * LANES // tok):
        q, off = divmod(w * tok, LANES)
        value = parts[q] if off == 0 else pltpu.roll(parts[q], LANES - off, 1)
        if off + tok > LANES:
            value = jnp.where(lane < LANES - off, value, pltpu.roll(parts[q + 1], LANES - off, 1))
        out.append(value)
    return out


def triangle_kernel(tok, blocks, x, out, xf, lhs, rhs, moved, of):
    devices = x.shape[0]
    share = out.shape[1] * LANES // (tok * tok)
    parts = 3
    groups = tok // 8
    kinds = 2 * share
    side_len = blocks * tok
    xf[...] = x[...].astype(F32).reshape(xf.shape)
    lane = lax.broadcasted_iota(jnp.int32, (tok, LANES), 1)
    per_block = devices // blocks * x.shape[1]

    def unpack(b, carry):
        cols = pl.ds(pl.multiple_of(b * LANES, LANES), LANES)
        for kind in range(kinds):
            side, e = divmod(kind, share)
            tiles = [
                xf[pl.ds(b * per_block + kind * parts + q, tok, stride=kinds * parts), :]
                for q in range(parts)
            ]
            for w, value in enumerate(windows_of(tiles, tok)):
                if side == 0:
                    rhs[e, w * tok : (w + 1) * tok, cols] = jnp.where(lane < tok, value, 0.0).astype(BF16)
                else:
                    lhs[e, w * tok : (w + 1) * tok, cols] = value.astype(BF16)
        return carry

    lax.fori_loop(0, blocks, unpack, 0, unroll=True)

    source = lax.broadcasted_iota(jnp.int32, (side_len, blocks * LANES), 0)
    target = lax.broadcasted_iota(jnp.int32, (side_len, blocks * LANES), 1)
    block, spot = target // LANES, target % LANES
    wanted = (spot % 8) * tok + block * groups + spot // 8
    place = jnp.where((source == wanted) & (spot < tok), 1.0, 0.0).astype(BF16)
    for e in range(share):
        product = nt(lhs[e], rhs[e]).astype(BF16)
        moved[e] = nn(product, place)

    def pack(b, carry):
        cols = pl.ds(pl.multiple_of(b * LANES, LANES), LANES)
        for e in range(share):
            tiles = [None] * parts
            for w in range(8):
                value = moved[e, w * tok : (w + 1) * tok, cols]
                q, off = divmod(w * tok, LANES)
                first = value if off == 0 else pltpu.roll(value, off, 1)
                tiles[q] = first if tiles[q] is None else jnp.where(lane >= off, first, tiles[q])
                if off + tok > LANES:
                    tiles[q + 1] = first
            for q in range(parts):
                at = b * blocks * out.shape[1] + e * parts + q
                of[pl.ds(at, tok, stride=share * parts), :] = tiles[q]
        return carry

    lax.fori_loop(0, blocks, pack, 0, unroll=True)
    out[...] = of[...].astype(BF16).reshape(out.shape)


def updated_group(g, each, devices, wide, gain, w_out, pair, gate):
    parts = 3
    share = w_out.shape[1] // devices
    tiles = [
        jnp.concatenate(
            [
                wide[pl.ds(g * share * parts + e * parts + q, devices, stride=each), :]
                for q in range(parts)
            ],
            axis=1,
        )
        for e in range(share)
    ]
    normed = norm(jnp.concatenate(tiles, axis=0), gain[...], 0).astype(BF16)
    return (pair[g].astype(F32) + gate[g] * nn(w_out[...], normed)).astype(BF16)


def middle_kernel(tri, pair, gate, gain_out, w_out, mask, gain, weights, w_gate, send, pair_new, gate_new, thin, wide, here, gates, sems):
    devices, each = tri.shape[0], tri.shape[1]
    groups = pair.shape[0]
    moves = [
        (
            pltpu.make_async_copy(pair.at[g], here.at[g], sems.at[0, g]),
            pltpu.make_async_copy(gate.at[g], gates.at[g], sems.at[1, g]),
        )
        for g in range(groups)
    ]
    for both in moves:
        for move in both:
            move.start()
    thin[...] = tri[...].astype(F32).reshape(thin.shape)
    for g in range(groups):
        for move in moves[g]:
            move.wait()
        block = updated_group(g, each, devices, thin, gain_out, w_out, here, gates)
        pair_new[g] = block
        normed = norm(block.astype(F32), gain[...], 0).astype(BF16)
        send_group(g, normed, weights[...], mask[pl.ds(g, 1), :], wide, devices)
        gate_new[g] = sigmoid(nn(w_gate[...], normed))
    send[...] = wide[...].astype(BF16).reshape(send.shape)


def last_kernel(tri, pair, gate, gain_out, w_out, gain, w_up, d_pair, grad, hidden, pair_new, thin, total, there, units, pairs, small, sems, outs):
    devices, each = tri.shape[0], tri.shape[1]
    groups, span = pair.shape[0], pair.shape[2]
    move = pltpu.make_async_copy(d_pair, there, sems.at[0])
    move.start()
    thin[...] = tri[...].astype(F32).reshape(thin.shape)
    expand = total.shape[0]
    leaving = []
    for g in range(groups):
        block = updated_group(g, each, devices, thin, gain_out, w_out, pair, gate)
        pairs[g] = block
        leaving.append(pltpu.make_async_copy(pairs.at[g], pair_new.at[g], outs.at[0, g]))
        normed = norm(block.astype(F32), gain[...], 0).astype(BF16)
        up = nn(w_up[...], normed)
        first = up[:expand]
        made = (first * sigmoid(first) * up[expand:]).astype(BF16)
        units[g] = made
        leaving.append(pltpu.make_async_copy(units.at[g], hidden.at[g], outs.at[1, g]))
        leaving[-2].start()
        leaving[-1].start()
        if g == 0:
            move.wait()
        part = nn(made, there[g * span : (g + 1) * span, :])
        total[...] = part if g == 0 else total[...] + part
    small[...] = total[...].astype(BF16)
    leaving.append(pltpu.make_async_copy(small, grad, sems.at[1]))
    leaving[-1].start()
    for copy in leaving:
        copy.wait()


def down_kernel(hidden, pair, w_down, out, wide):
    tok = out.shape[0]

    def group(g, carry):
        result = (pair[g].astype(F32) + nn(w_down[...], hidden[g])).T
        for n in range(8):
            wide[pl.ds(g * 8 + n, tok, stride=tok), :] = result[n * tok : (n + 1) * tok]
        return carry

    lax.fori_loop(0, hidden.shape[0], group, 0)
    out[...] = wide[...].astype(BF16).reshape(out.shape)


def call(kernel, outs, scratch, name, cost, *args, far=(), far_out=(), scalar=(), scalar_out=()):
    space = [
        pltpu.SMEM if n in scalar else pltpu.HBM if n in far else pltpu.VMEM for n in range(len(args))
    ]
    args = [
        pltpu.with_memory_space_constraint(arg, pltpu.HBM) if n in far else arg
        for n, arg in enumerate(args)
    ]
    many = isinstance(outs, tuple)
    out_space = [
        pltpu.HBM if n in far_out else pltpu.SMEM if n in scalar_out else pltpu.VMEM for n in range(len(outs) if many else 1)
    ]
    out_specs = tuple(pl.BlockSpec(memory_space=s) for s in out_space)
    listed = [
        pltpu.HBM(o.shape, o.dtype) if n in far_out else o
        for n, o in enumerate(outs if many else (outs,))
    ]
    outs = tuple(listed) if many else listed[0]
    return pl.pallas_call(
        kernel,
        out_shape=outs,
        in_specs=[pl.BlockSpec(memory_space=s) for s in space],
        out_specs=out_specs if many else out_specs[0],
        scratch_shapes=scratch,
        compiler_params=PARAMS,
        name=name,
        cost_estimate=pl.CostEstimate(flops=cost, bytes_accessed=4 * 2**20, transcendentals=10**6),
    )(*args)


def local(
    atom_feats,
    atom_token,
    atom_counts,
    restype,
    pair_in,
    pair_mask,
    w_atom,
    w_restype,
    w_pair,
    ln_tri,
    w_tri_in,
    ln_tri_out,
    w_tri_out,
    ln_trans,
    w_up,
    w_down,
    d_pair,
):
    n_row, n_col = lax.axis_size("row"), lax.axis_size("col")
    devices = n_row * n_col
    tok = pair_in.shape[1]
    width = pair_in.shape[3]
    inner = w_tri_out.shape[1]
    expand = w_down.shape[0]
    share = inner // devices
    count = tok * tok
    groups = tok // 8
    span = 8 * tok

    shape = jax.ShapeDtypeStruct
    cost = 400 * 10**6
    feats = call(
        spread_kernel,
        shape((devices,) + atom_feats.shape[1:], BF16),
        [pltpu.VMEM((n_col,) + atom_feats.shape[1:], BF16), pltpu.SemaphoreType.DMA((n_row,))],
        "spread",
        cost // 100,
        atom_feats[0],
        far_out=(0,),
    )
    feats = exchange(feats, ("row", "col")).reshape(-1, atom_feats.shape[-1])

    plain, tokens, bounds = call(
        prepare_kernel,
        (
            shape((groups, width, span), BF16),
            shape((2 * tok, 4), jnp.int32),
            shape((4,), jnp.int32),
        ),
        [
            pltpu.VMEM((count, width), F32),
            pltpu.VMEM((groups, width, span), BF16),
            pltpu.SemaphoreType.DMA,
        ],
        "prepare",
        cost,
        jnp.stack([lax.axis_index("row"), lax.axis_index("col")]).astype(jnp.int32),
        pair_in[0],
        atom_counts,
        restype,
        far_out=(0,),
        scalar=(0,),
        scalar_out=(2,),
    )
    valid = pair_mask[0].astype(F32)
    mask = valid.reshape(groups, span)

    def column(gain):
        return jnp.broadcast_to(gain[:, None], (gain.shape[0], span))

    def side_weights(weights):
        blocks = weights[:, : 4 * inner].reshape(width, 2, 2, devices, share)
        return blocks.transpose(2, 1, 4, 3, 0).reshape(4 * inner, width)

    def by_owner(values, update):
        if update == 0:
            order = values.reshape((n_col, n_row, share) + values.shape[1:]).swapaxes(0, 1)
        else:
            order = values.reshape((n_row, n_col, share) + values.shape[1:])
        return jnp.moveaxis(order, 2, 0).reshape(values.shape)

    rows_out = 2 * share * count // LANES
    rows_back = share * count // LANES
    send_shape = shape((devices, rows_out, LANES), BF16)
    back_shape = shape((devices, rows_back, LANES), BF16)
    wide = pltpu.VMEM((devices * rows_out, LANES), F32)
    thin = pltpu.VMEM((devices * rows_back, LANES), F32)
    flat = shape((groups, width, span), BF16)
    flat_wide = shape((groups, width, span), F32)
    here = pltpu.VMEM(flat.shape, BF16)
    gates = pltpu.VMEM(flat.shape, F32)

    def triangle(value):
        blocks = n_row
        return call(
            functools.partial(triangle_kernel, tok, blocks),
            back_shape,
            [
                wide,
                pltpu.VMEM((share, blocks * tok, blocks * LANES), BF16),
                pltpu.VMEM((share, blocks * tok, blocks * LANES), BF16),
                pltpu.VMEM((share, blocks * tok, blocks * LANES), F32),
                thin,
            ],
            "triangle",
            cost,
            value,
        )

    send, sides = call(
        front_kernel,
        (send_shape, shape((width, 2 * tok), BF16)),
        [wide, here, pltpu.SemaphoreType.DMA],
        "front",
        cost,
        bounds,
        feats,
        tokens,
        w_atom,
        w_restype,
        w_pair,
        plain,
        mask,
        column(ln_tri[0]),
        side_weights(w_tri_in[0]),
        far=(6,),
        scalar=(0,),
    )
    arrived = exchange(send, ("col", "row"))
    arrived, sides, pair_in, d_pair, valid, w_tri_in, w_tri_out, ln_tri, ln_tri_out, w_up, w_down, ln_trans = (
        lax.optimization_barrier(
            (arrived, sides, pair_in, d_pair, valid, w_tri_in, w_tri_out, ln_tri, ln_tri_out, w_up, w_down, ln_trans)
        )
    )
    tri = exchange(triangle(arrived), ("row", "col"))
    w_gates = w_tri_in[:, :, 4 * inner :].swapaxes(1, 2)
    w_outs = [by_owner(w_tri_out[u], u).T for u in range(2)]
    gains_out = [column(by_owner(ln_tri_out[u], u)) for u in range(2)]
    pair, gate = call(
        first_gate_kernel,
        (flat, flat_wide),
        [pltpu.VMEM((count, width), F32), here, gates, pltpu.SemaphoreType.DMA((2,))],
        "first_gate",
        cost,
        pair_in[0],
        sides,
        column(ln_tri[0]),
        w_gates[0],
        far_out=(0, 1),
    )
    turned_grad = call(
        turn_kernel,
        shape((count, width), BF16),
        [pltpu.VMEM((count, width), F32), pltpu.VMEM((count, width), BF16), pltpu.SemaphoreType.DMA],
        "turn",
        cost,
        d_pair[0],
        far_out=(0,),
    )
    late = [gains_out[1], w_outs[1], column(ln_trans), w_up.T, w_down.T, turned_grad]
    ready = [
        gains_out[0],
        w_outs[0],
        valid.T.reshape(groups, span),
        column(ln_tri[1]),
        side_weights(w_tri_in[1]),
        w_gates[1],
    ]
    ready, late = lax.optimization_barrier((ready, late))
    send, pair, gate = call(
        middle_kernel,
        (send_shape, flat, flat_wide),
        [thin, wide, here, gates, pltpu.SemaphoreType.DMA((2, groups))],
        "middle",
        cost,
        tri,
        pair,
        gate,
        *ready,
        far=(1, 2),
    )
    arrived = exchange(send, ("row", "col"))
    tri = exchange(triangle(arrived), ("row", "col"))
    grad, hidden, pair = call(
        last_kernel,
        (shape((expand, width), BF16), shape((groups, expand, span), BF16), flat),
        [
            thin,
            pltpu.VMEM((expand, width), F32),
            pltpu.VMEM((count, width), BF16),
            pltpu.VMEM((groups, expand, span), BF16),
            here,
            pltpu.VMEM((expand, width), BF16),
            pltpu.SemaphoreType.DMA((2,)),
            pltpu.SemaphoreType.DMA((2, groups)),
        ],
        "last",
        2 * cost,
        tri,
        pair,
        gate,
        late[0],
        late[1],
        late[2],
        late[3],
        late[5],
        far=(7,),
        far_out=(0, 1, 2),
    )
    everyone = devices * lax.axis_size("rep")
    grad = exchange(grad.reshape(everyone, expand // everyone, width), ("row", "col", "rep"))
    result = call(
        down_kernel,
        shape((tok, tok, width), BF16),
        [pltpu.VMEM((count, width), F32)],
        "down",
        cost,
        hidden,
        pair,
        late[4],
    )
    return (result[None], jnp.sum(grad.astype(F32), axis=0))


def solution(mesh):
    return jax.shard_map(
        local,
        mesh=mesh,
        in_specs=(
            P("rep", ("row", "col"), None),
            P("rep", ("row", "col")),
            P("rep", None),
            P("rep", None),
            P("rep", "row", "col", None),
            P("rep", "row", "col"),
            P(),
            P(),
            P(),
            P(),
            P(),
            P(),
            P(),
            P(),
            P(),
            P(),
            P("rep", "row", "col", None),
        ),
        out_specs=(P("rep", "row", "col", None), P(("row", "col", "rep"), None)),
        check_vma=False,
    )
```

```python
import functools

import jax
import jax.numpy as jnp
from jax import lax
from jax.experimental import pallas as pl
from jax.experimental.pallas import tpu as pltpu
from jax.sharding import Mesh, PartitionSpec as P

F32, BF16 = jnp.float32, jnp.bfloat16
LANES = 128
ROW, COL = ("x", "core"), ("y", "zl")
TOGETHER = 2
PARAMS = pltpu.CompilerParams(vmem_limit_bytes=20 * 2**20)


def nt(a, b):
    return lax.dot_general(a, b, (((1,), (1,)), ((), ())), preferred_element_type=F32)


def nn(a, b):
    return lax.dot_general(a, b, (((1,), (0,)), ((), ())), preferred_element_type=F32)


def norm(values, scales, axis):
    average = jnp.mean(values, axis=axis, keepdims=True)
    centred = values - average
    variance = jnp.mean(centred * centred, axis=axis, keepdims=True)
    return centred * lax.rsqrt(variance + 1e-05) * scales


def sigmoid(x):
    return jax.nn.sigmoid(x)


def exchange(value, axes):
    return lax.all_to_all(value, axes, 0, 0, tiled=True)


def send_groups(first, normed, weights, mask, wide, devices):
    proj = nn(weights, normed)
    half = proj.shape[0] // 2
    span = mask.shape[1]
    count = proj.shape[1] // span
    valid = jnp.concatenate([mask[pl.ds(first + n, 1), :] for n in range(count)], axis=1)
    sides = sigmoid(proj[:half]) * proj[half:] * valid
    rows = wide.shape[0] // devices
    parts = span // LANES
    kinds = half // devices
    for n in range(count):
        for kind in range(kinds):
            for q in range(parts):
                at = n * span + q * LANES
                wide[pl.ds(((first + n) * kinds + kind) * parts + q, devices, stride=rows), :] = sides[
                    kind * devices : (kind + 1) * devices, at : at + LANES
                ]


def beside(array, first):
    return jnp.concatenate([array[first + n] for n in range(TOGETHER)], axis=1)


def widened(gain):
    return jnp.concatenate([gain[...]] * TOGETHER, axis=1)


def apart(array, first, value):
    span = value.shape[1] // TOGETHER
    for n in range(TOGETHER):
        array[first + n] = value[:, n * span : (n + 1) * span]


def spread_kernel(value, out, copies, sems):
    several = copies.shape[0]
    copies[...] = jnp.broadcast_to(value[...], copies.shape)
    moves = [
        pltpu.make_async_copy(copies, out.at[pl.ds(n * several, several)], sems.at[n])
        for n in range(out.shape[0] // several)
    ]
    for move in moves:
        move.start()
    for move in moves:
        move.wait()


def prepare_kernel(chunk, place, pair_in, counts, types, w_restype, plain, tokens, bounds, chosen, embedded, wide, made, sem):
    tok, width = pair_in.shape[0], pair_in.shape[2]
    span = 8 * tok
    wide[...] = pair_in[...].astype(F32).reshape(wide.shape)

    def turn(g, carry):
        rows = pl.ds(pl.multiple_of(g * span, span), span)
        made[g] = wide[rows, :].T.astype(BF16)
        return carry

    lax.fori_loop(0, tok // 8, turn, 0)
    move = pltpu.make_async_copy(made, plain, sem)
    move.start()
    shape = (2 * tok, counts.shape[1])
    slot = lax.broadcasted_iota(jnp.int32, shape, 0)
    mine = jnp.where(slot < tok, place[0] * tok + slot, place[1] * tok + slot - tok)
    token = lax.broadcasted_iota(jnp.int32, shape, 1)
    numbers = jnp.broadcast_to(counts[...].astype(F32), shape)
    kinds = jnp.broadcast_to(types[...].astype(F32), shape)

    def total(wanted, values):
        return jnp.sum(jnp.where(wanted, values, 0.0), axis=1, keepdims=True)

    columns = [
        total(token < mine, numbers),
        total(token <= mine, numbers),
        total(token == mine, numbers),
        total(token == mine, kinds),
    ]
    kind = lax.broadcasted_iota(jnp.int32, (2 * tok, w_restype.shape[0]), 1)
    picked = jnp.where(kind == columns[3].astype(jnp.int32), 1.0, 0.0).astype(BF16)
    embedded[...] = nn(picked, w_restype[...])
    lane = lax.broadcasted_iota(jnp.int32, tokens.shape, 1)
    table = jnp.zeros(tokens.shape, F32)
    for n, column in enumerate(columns):
        table = jnp.where(lane == n, column, table)
    tokens[...] = table.astype(jnp.int32)
    every = lax.broadcasted_iota(jnp.int32, counts.shape, 1)
    for k in range(2):
        first = place[k] * tok
        start = jnp.sum(jnp.where(every < first, counts[...], 0))
        end = jnp.sum(jnp.where(every < first + tok, counts[...], 0))
        bounds[2 * k] = start // chunk
        bounds[2 * k + 1] = (end + chunk - 1) // chunk
    bounds[4] = place[0] % 2
    for g in range(tok // 8):
        chosen[g] = choice(g, tok, False)
    move.wait()


def turned_rows(g, source, tok):
    rows = [source[pl.ds(g * 8 + n, tok, stride=tok), :] for n in range(8)]
    return jnp.concatenate(rows, axis=0)


def turn_kernel(d_pair, out, wide, made, sem):
    tok = d_pair.shape[0]
    span = 8 * tok
    wide[...] = d_pair[...].astype(F32).reshape(wide.shape)

    def grads(g, carry):
        rows = pl.ds(pl.multiple_of(g * span, span), span)
        made[rows, :] = turned_rows(g, wide, tok).astype(BF16)
        return carry

    lax.fori_loop(0, tok // 8, grads, 0)
    move = pltpu.make_async_copy(made, out, sem)
    move.start()
    move.wait()


def choice(g, tok, turned):
    shape = (2 * tok, 8 * tok)
    source = lax.broadcasted_iota(jnp.int32, shape, 0)
    token = lax.broadcasted_iota(jnp.int32, shape, 1)
    high, low = g * 8 + token // tok, token % tok
    left, right = (low, high) if turned else (high, low)
    wanted = (source == left) | (source == right + tok)
    return jnp.where(wanted, 1.0, 0.0).astype(BF16)


def front_kernel(bounds, same, other, tokens, embedded, w_atom, w_pair, plain, chosen, mask, gain, weights, send, sides, wide, feats, pair_in, sem):
    groups, width, span = plain.shape
    tok = span // 8
    devices = send.shape[0]
    move = pltpu.make_async_copy(plain, pair_in, sem)
    move.start()
    chunks, chunk = feats.shape[0], feats.shape[1]
    for n in range(chunks // 2):
        feats[2 * n + bounds[4]] = same[n * chunk : (n + 1) * chunk, :]
        feats[2 * n + 1 - bounds[4]] = other[n * chunk : (n + 1) * chunk, :]

    def pool(n, sums):
        out = []
        for k in range(2):
            q = bounds[2 * k] + n
            act = jnp.maximum(nn(feats[jnp.minimum(q, chunks - 1)], w_atom[...]), 0.0).astype(BF16)
            atoms = lax.broadcasted_iota(jnp.int32, (tok, chunk), 1) + q * chunk
            starts = tokens[k * tok : (k + 1) * tok, 0:1]
            ends = tokens[k * tok : (k + 1) * tok, 1:2]
            mine = (atoms >= starts) & (atoms < ends)
            out.append(sums[k] + nn(jnp.where(mine, 1.0, 0.0).astype(BF16), act))
        return tuple(out)

    steps = jnp.maximum(bounds[1] - bounds[0], bounds[3] - bounds[2])
    zero = jnp.zeros((tok, w_atom.shape[1]), F32)
    sums = lax.fori_loop(0, steps, pool, (zero, zero))
    counts = tokens[:, 2:3].astype(F32)
    single = (jnp.concatenate(sums, 0) / counts + embedded[...]).astype(BF16)
    left = nn(single[:tok], w_pair[:, :width])
    right = nn(single[tok:], w_pair[:, width:])
    sides[...] = jnp.concatenate([left, right], 0).T.astype(BF16)
    move.wait()

    for g in range(0, groups, TOGETHER):
        block = beside(pair_in, g).astype(F32) + nn(sides[...], beside(chosen, g))
        normed = norm(block.astype(BF16).astype(F32), widened(gain), 0).astype(BF16)
        send_groups(g, normed, weights[...], mask, wide, devices)
    send[...] = wide[...].astype(BF16).reshape(send.shape)


def first_gate_kernel(pair_in, sides, gain, w_gate, pair_out, gate_out, wide, pair, gate, sems):
    tok = pair_in.shape[0]
    wide[...] = pair_in[...].astype(F32).reshape(wide.shape)

    def group(g, carry):
        block = turned_rows(g, wide, tok).T + nn(sides[...], choice(g, tok, True))
        block = block.astype(BF16)
        pair[g] = block
        normed = norm(block.astype(F32), gain[...], 0).astype(BF16)
        gate[g] = sigmoid(nn(w_gate[...], normed)).astype(BF16)
        return carry

    lax.fori_loop(0, tok // 8, group, 0)
    moves = [
        pltpu.make_async_copy(pair, pair_out, sems.at[0]),
        pltpu.make_async_copy(gate, gate_out, sems.at[1]),
    ]
    for move in moves:
        move.start()
    for move in moves:
        move.wait()


def windows_of(parts, tok, start):
    lane = lax.broadcasted_iota(jnp.int32, parts[0].shape, 1)
    out = []
    for w in range(len(parts) * LANES // tok):
        q, off = divmod(w * tok, LANES)
        turn = (start - off) % LANES
        value = parts[q] if turn == 0 else pltpu.roll(parts[q], turn, 1)
        if off + tok > LANES:
            rest = parts[q + 1] if turn == 0 else pltpu.roll(parts[q + 1], turn, 1)
            value = jnp.where(lane < start + LANES - off, value, rest)
        out.append(value)
    return out


def triangle_kernel(tok, blocks, x, out, xf, lhs, rhs, moved, of):
    devices = x.shape[0]
    share = out.shape[1] * LANES // (tok * tok)
    parts = 3
    groups = tok // 8
    kinds = 2 * share
    side_len = blocks * tok
    xf[...] = x[...].astype(F32).reshape(xf.shape)
    lane = lax.broadcasted_iota(jnp.int32, (tok, LANES), 1)
    per_block = devices // blocks * x.shape[1]

    half = LANES // 2
    used = lane % half < tok
    for b in range(0, blocks, 2):
        cols = slice(b * half, b * half + LANES)
        for kind in range(kinds):
            side, e = divmod(kind, share)
            pairs = []
            for n in range(2):
                tiles = [
                    xf[pl.ds((b + n) * per_block + kind * parts + q, tok, stride=kinds * parts), :]
                    for q in range(parts)
                ]
                pairs.append(windows_of(tiles, tok, n * half))
            for w in range(8):
                value = jnp.where(lane < half, pairs[0][w], pairs[1][w])
                rows = slice(w * tok, (w + 1) * tok)
                if side == 0:
                    rhs[e, rows, cols] = jnp.where(used, value, 0.0).astype(BF16)
                else:
                    lhs[e, rows, cols] = value.astype(BF16)

    width = blocks * half
    source = lax.broadcasted_iota(jnp.int32, (side_len, width), 0)
    target = lax.broadcasted_iota(jnp.int32, (side_len, width), 1)
    block, spot = target // half, target % half
    wanted = (spot % 8) * tok + block * groups + spot // 8
    place = jnp.where((source == wanted) & (spot < tok), 1.0, 0.0).astype(BF16)
    for e in range(share):
        product = nt(lhs[e], rhs[e]).astype(BF16)
        moved[e] = nn(product, place)

    for b in range(blocks):
        at, start = b // 2 * LANES, b % 2 * half
        for e in range(share):
            tiles = [None] * parts
            for w in range(8):
                value = moved[e, w * tok : (w + 1) * tok, at : at + LANES]
                q, off = divmod(w * tok, LANES)
                turn = (off - start) % LANES
                first = value if turn == 0 else pltpu.roll(value, turn, 1)
                tiles[q] = first if tiles[q] is None else jnp.where(lane >= off, first, tiles[q])
                if off + tok > LANES:
                    tiles[q + 1] = first
            for q in range(parts):
                base = b * blocks * out.shape[1] + e * parts + q
                of[pl.ds(base, tok, stride=share * parts), :] = tiles[q]
    out[...] = of[...].astype(BF16).reshape(out.shape)


def updated_groups(first, each, devices, wide, gain, w_out, pair, gate):
    parts = 3
    share = w_out.shape[1] // devices
    tiles = [
        jnp.concatenate(
            [
                wide[pl.ds((g * share + e) * parts + q, devices, stride=each), :]
                for g in range(first, first + TOGETHER)
                for q in range(parts)
            ],
            axis=1,
        )
        for e in range(share)
    ]
    normed = norm(jnp.concatenate(tiles, axis=0), widened(gain), 0).astype(BF16)
    change = beside(gate, first).astype(F32) * nn(w_out[...], normed)
    return (beside(pair, first).astype(F32) + change).astype(BF16)


def middle_kernel(tri, pair, gate, gain_out, w_out, mask, gain, weights, w_gate, send, pair_new, gate_new, thin, wide, here, gates, sems):
    devices, each = tri.shape[0], tri.shape[1]
    groups = pair.shape[0]
    moves = [
        (
            pltpu.make_async_copy(pair.at[g], here.at[g], sems.at[0, g]),
            pltpu.make_async_copy(gate.at[g], gates.at[g], sems.at[1, g]),
        )
        for g in range(groups)
    ]
    for both in moves:
        for move in both:
            move.start()
    thin[...] = tri[...].astype(F32).reshape(thin.shape)
    for g in range(0, groups, TOGETHER):
        for both in moves[g : g + TOGETHER]:
            for move in both:
                move.wait()
        block = updated_groups(g, each, devices, thin, gain_out, w_out, here, gates)
        apart(pair_new, g, block)
        normed = norm(block.astype(F32), widened(gain), 0).astype(BF16)
        send_groups(g, normed, weights[...], mask, wide, devices)
        apart(gate_new, g, sigmoid(nn(w_gate[...], normed)).astype(BF16))
    send[...] = wide[...].astype(BF16).reshape(send.shape)


def last_kernel(tri, pair, gate, gain_out, w_out, gain, w_up, d_pair, grad, hidden, pair_new, thin, total, there, units, pairs, small, sems, outs):
    devices, each = tri.shape[0], tri.shape[1]
    groups, span = pair.shape[0], pair.shape[2]
    move = pltpu.make_async_copy(d_pair, there, sems.at[0])
    move.start()
    thin[...] = tri[...].astype(F32).reshape(thin.shape)
    expand = total.shape[0]
    leaving = []
    for g in range(0, groups, TOGETHER):
        block = updated_groups(g, each, devices, thin, gain_out, w_out, pair, gate)
        apart(pairs, g, block)
        normed = norm(block.astype(F32), widened(gain), 0).astype(BF16)
        up = nn(w_up[...], normed)
        first = up[:expand]
        made = (first * sigmoid(first) * up[expand:]).astype(BF16)
        apart(units, g, made)
        for n in range(g, g + TOGETHER):
            for copy in (
                pltpu.make_async_copy(pairs.at[n], pair_new.at[n], outs.at[0, n]),
                pltpu.make_async_copy(units.at[n], hidden.at[n], outs.at[1, n]),
            ):
                copy.start()
                leaving.append(copy)
        if g == 0:
            move.wait()
        part = nn(made, there[g * span : (g + TOGETHER) * span, :])
        total[...] = part if g == 0 else total[...] + part
    small[...] = total[...].astype(BF16)
    leaving.append(pltpu.make_async_copy(small, grad, sems.at[1]))
    leaving[-1].start()
    for copy in leaving:
        copy.wait()


def down_kernel(hidden, pair, w_down, out, wide):
    tok = out.shape[0]

    def group(g, carry):
        result = (pair[g].astype(F32) + nn(w_down[...], hidden[g])).T
        for n in range(8):
            wide[pl.ds(g * 8 + n, tok, stride=tok), :] = result[n * tok : (n + 1) * tok]
        return carry

    lax.fori_loop(0, hidden.shape[0], group, 0)
    out[...] = wide[...].astype(BF16).reshape(out.shape)


def call(kernel, outs, scratch, name, cost, *args, far=(), far_out=(), scalar=(), scalar_out=()):
    space = [
        pltpu.SMEM if n in scalar else pltpu.HBM if n in far else pltpu.VMEM for n in range(len(args))
    ]
    args = [
        pltpu.with_memory_space_constraint(arg, pltpu.HBM) if n in far else arg
        for n, arg in enumerate(args)
    ]
    many = isinstance(outs, tuple)
    out_space = [
        pltpu.HBM if n in far_out else pltpu.SMEM if n in scalar_out else pltpu.VMEM for n in range(len(outs) if many else 1)
    ]
    out_specs = tuple(pl.BlockSpec(memory_space=s) for s in out_space)
    listed = [
        pltpu.HBM(o.shape, o.dtype) if n in far_out else o
        for n, o in enumerate(outs if many else (outs,))
    ]
    outs = tuple(listed) if many else listed[0]
    return pl.pallas_call(
        kernel,
        out_shape=outs,
        in_specs=[pl.BlockSpec(memory_space=s) for s in space],
        out_specs=out_specs if many else out_specs[0],
        scratch_shapes=scratch,
        compiler_params=PARAMS,
        name=name,
        cost_estimate=pl.CostEstimate(flops=cost, bytes_accessed=4 * 2**20, transcendentals=10**6),
    )(*args)


def local(
    atom_feats,
    atom_token,
    atom_counts,
    restype,
    pair_in,
    pair_mask,
    w_atom,
    w_restype,
    w_pair,
    ln_tri,
    w_tri_in,
    ln_tri_out,
    w_tri_out,
    ln_trans,
    w_up,
    w_down,
    d_pair,
):
    n_row, n_col = lax.axis_size(ROW), lax.axis_size(COL)
    devices = n_row * n_col
    tok = pair_in.shape[1]
    width = pair_in.shape[3]
    inner = w_tri_out.shape[1]
    expand = w_down.shape[0]
    share = inner // devices
    count = tok * tok
    groups = tok // 8
    span = 8 * tok

    shape = jax.ShapeDtypeStruct
    cost = 400 * 10**6
    half = devices // 2
    spread = call(
        spread_kernel,
        shape((half,) + atom_feats.shape[1:], BF16),
        [pltpu.VMEM((n_row,) + atom_feats.shape[1:], BF16), pltpu.SemaphoreType.DMA((half // n_row,))],
        "spread",
        cost // 100,
        atom_feats[0],
        far_out=(0,),
    )
    same = exchange(spread, ("x", "y", "zl")).reshape(-1, atom_feats.shape[-1])

    plain, tokens, bounds, chosen, embedded = call(
        functools.partial(prepare_kernel, n_col * atom_feats.shape[1]),
        (
            shape((groups, width, span), BF16),
            shape((2 * tok, 4), jnp.int32),
            shape((5,), jnp.int32),
            shape((groups, 2 * tok, span), BF16),
            shape((2 * tok, w_restype.shape[1]), F32),
        ),
        [
            pltpu.VMEM((count, width), F32),
            pltpu.VMEM((groups, width, span), BF16),
            pltpu.SemaphoreType.DMA,
        ],
        "prepare",
        cost,
        jnp.stack([lax.axis_index(ROW), lax.axis_index(COL)]).astype(jnp.int32),
        pair_in[0],
        atom_counts,
        restype,
        w_restype,
        far_out=(0,),
        scalar=(0,),
        scalar_out=(2,),
    )
    same, bounds = lax.optimization_barrier((same, bounds))
    other = lax.ppermute(same, "core", [(0, 1), (1, 0)])
    valid = pair_mask[0].astype(F32)
    mask = valid.reshape(groups, span)

    def column(gain):
        return jnp.broadcast_to(gain[:, None], (gain.shape[0], span))

    def side_weights(weights):
        blocks = weights[:, : 4 * inner].reshape(width, 2, 2, devices, share)
        return blocks.transpose(2, 1, 4, 3, 0).reshape(4 * inner, width)

    def by_owner(values, update):
        if update == 0:
            order = values.reshape((n_col, n_row, share) + values.shape[1:]).swapaxes(0, 1)
        else:
            order = values.reshape((n_row, n_col, share) + values.shape[1:])
        return jnp.moveaxis(order, 2, 0).reshape(values.shape)

    rows_out = 2 * share * count // LANES
    rows_back = share * count // LANES
    send_shape = shape((devices, rows_out, LANES), BF16)
    back_shape = shape((devices, rows_back, LANES), BF16)
    wide = pltpu.VMEM((devices * rows_out, LANES), F32)
    thin = pltpu.VMEM((devices * rows_back, LANES), F32)
    flat = shape((groups, width, span), BF16)
    here = pltpu.VMEM(flat.shape, BF16)
    gates = here

    def triangle(value):
        blocks = n_row
        return call(
            functools.partial(triangle_kernel, tok, blocks),
            back_shape,
            [
                wide,
                pltpu.VMEM((share, blocks * tok, blocks * LANES // 2), BF16),
                pltpu.VMEM((share, blocks * tok, blocks * LANES // 2), BF16),
                pltpu.VMEM((share, blocks * tok, blocks * LANES // 2), F32),
                thin,
            ],
            "triangle",
            cost,
            value,
        )

    send, sides = call(
        front_kernel,
        (send_shape, shape((width, 2 * tok), BF16)),
        [wide, pltpu.VMEM((n_row, n_col * atom_feats.shape[1], atom_feats.shape[2]), BF16), here, pltpu.SemaphoreType.DMA],
        "front",
        cost,
        bounds,
        same,
        other,
        tokens,
        embedded,
        w_atom,
        w_pair,
        plain,
        chosen,
        mask,
        column(ln_tri[0]),
        side_weights(w_tri_in[0]),
        far=(7,),
        scalar=(0,),
    )
    arrived = exchange(send, COL + ROW)
    arrived, sides, pair_in, d_pair, valid, w_tri_in, w_tri_out, ln_tri, ln_tri_out, w_up, w_down, ln_trans = (
        lax.optimization_barrier(
            (arrived, sides, pair_in, d_pair, valid, w_tri_in, w_tri_out, ln_tri, ln_tri_out, w_up, w_down, ln_trans)
        )
    )
    tri = exchange(triangle(arrived), ROW + COL)
    w_gates = w_tri_in[:, :, 4 * inner :].swapaxes(1, 2)
    w_outs = [by_owner(w_tri_out[u], u).T for u in range(2)]
    gains_out = [column(by_owner(ln_tri_out[u], u)) for u in range(2)]
    pair, gate = call(
        first_gate_kernel,
        (flat, flat),
        [pltpu.VMEM((count, width), F32), here, gates, pltpu.SemaphoreType.DMA((2,))],
        "first_gate",
        cost,
        pair_in[0],
        sides,
        column(ln_tri[0]),
        w_gates[0],
        far_out=(0, 1),
    )
    turned_grad = call(
        turn_kernel,
        shape((count, width), BF16),
        [pltpu.VMEM((count, width), F32), pltpu.VMEM((count, width), BF16), pltpu.SemaphoreType.DMA],
        "turn",
        cost,
        d_pair[0],
        far_out=(0,),
    )
    late = [gains_out[1], w_outs[1], column(ln_trans), w_up.T, w_down.T, turned_grad]
    ready = [
        gains_out[0],
        w_outs[0],
        valid.T.reshape(groups, span),
        column(ln_tri[1]),
        side_weights(w_tri_in[1]),
        w_gates[1],
    ]
    ready, late = lax.optimization_barrier((ready, late))
    send, pair, gate = call(
        middle_kernel,
        (send_shape, flat, flat),
        [thin, wide, here, gates, pltpu.SemaphoreType.DMA((2, groups))],
        "middle",
        cost,
        tri,
        pair,
        gate,
        *ready,
        far=(1, 2),
    )
    arrived = exchange(send, ROW + COL)
    tri = exchange(triangle(arrived), ROW + COL)
    grad, hidden, pair = call(
        last_kernel,
        (shape((expand, width), BF16), shape((groups, expand, span), BF16), flat),
        [
            thin,
            pltpu.VMEM((expand, width), F32),
            pltpu.VMEM((count, width), BF16),
            pltpu.VMEM((groups, expand, span), BF16),
            here,
            pltpu.VMEM((expand, width), BF16),
            pltpu.SemaphoreType.DMA((2,)),
            pltpu.SemaphoreType.DMA((2, groups)),
        ],
        "last",
        2 * cost,
        tri,
        pair,
        gate,
        late[0],
        late[1],
        late[2],
        late[3],
        late[5],
        far=(7,),
        far_out=(0, 1, 2),
    )
    everyone = devices * lax.axis_size("rep")
    grad = exchange(grad.reshape(everyone, expand // everyone, width), ROW + COL + ("rep",))
    result = call(
        down_kernel,
        shape((tok, tok, width), BF16),
        [pltpu.VMEM((count, width), F32)],
        "down",
        cost,
        hidden,
        pair,
        late[4],
    )
    return (result[None], jnp.sum(grad.astype(F32), axis=0))


def solution(mesh):
    rows, cols, reps = (mesh.shape[name] for name in ("row", "col", "rep"))
    parts = Mesh(
        mesh.devices.reshape(rows // 2, 2, cols // 2, 2, reps), ROW + COL + ("rep",)
    )
    pair = P("rep", ROW, COL, None)
    return jax.shard_map(
        local,
        mesh=parts,
        in_specs=(
            P("rep", ROW + COL, None),
            P("rep", ROW + COL),
            P("rep", None),
            P("rep", None),
            pair,
            P("rep", ROW, COL),
            *[P()] * 10,
            pair,
        ),
        out_specs=(pair, P(ROW + COL + ("rep",), None)),
        check_vma=False,
    )
```

```python
import functools

import jax
import jax.numpy as jnp
from jax import lax
from jax.experimental import pallas as pl
from jax.experimental.pallas import tpu as pltpu
from jax.sharding import Mesh, PartitionSpec as P

F32, BF16 = jnp.float32, jnp.bfloat16
LANES = 128
ROW, COL = ("x", "core"), ("y", "zl")
FRONT, LATE = 6, 3
PARAMS = pltpu.CompilerParams(vmem_limit_bytes=32 * 2**20)


def nt(a, b):
    return lax.dot_general(a, b, (((1,), (1,)), ((), ())), preferred_element_type=F32)


def nn(a, b):
    return lax.dot_general(a, b, (((1,), (0,)), ((), ())), preferred_element_type=F32)


def norm(values, scales, axis):
    average = jnp.mean(values, axis=axis, keepdims=True)
    centred = values - average
    variance = jnp.mean(centred * centred, axis=axis, keepdims=True)
    return centred * lax.rsqrt(variance + 1e-05) * scales


def sigmoid(x):
    return jax.nn.sigmoid(x)


def exchange(value, axes):
    return lax.all_to_all(value, axes, 0, 0, tiled=True)


def send_groups(first, normed, weights, mask, wide, devices):
    proj = nn(weights, normed)
    half = proj.shape[0] // 2
    span = mask.shape[1]
    count = proj.shape[1] // span
    valid = jnp.concatenate([mask[pl.ds(first + n, 1), :] for n in range(count)], axis=1)
    sides = sigmoid(proj[:half]) * proj[half:] * valid
    rows = wide.shape[0] // devices
    parts = span // LANES
    kinds = half // devices
    for n in range(count):
        for kind in range(kinds):
            for q in range(parts):
                at = n * span + q * LANES
                wide[pl.ds(((first + n) * kinds + kind) * parts + q, devices, stride=rows), :] = sides[
                    kind * devices : (kind + 1) * devices, at : at + LANES
                ]


def beside(array, first, count):
    return jnp.concatenate([array[first + n] for n in range(count)], axis=1)


def widened(gain, count):
    return jnp.concatenate([gain[...]] * count, axis=1)


def apart(array, first, value):
    span = array.shape[2]
    for n in range(value.shape[1] // span):
        array[first + n] = value[:, n * span : (n + 1) * span]


def prepare_kernel(chunk, place, pair_in, counts, types, w_restype, plain, tokens, bounds, chosen, embedded, wide, made, sem):
    tok, width = pair_in.shape[0], pair_in.shape[2]
    span = 8 * tok
    wide[...] = pair_in[...].astype(F32).reshape(wide.shape)

    def turn(g, carry):
        rows = pl.ds(pl.multiple_of(g * span, span), span)
        made[g] = wide[rows, :].T.astype(BF16)
        return carry

    lax.fori_loop(0, tok // 8, turn, 0)
    move = pltpu.make_async_copy(made, plain, sem)
    move.start()
    shape = (2 * tok, counts.shape[1])
    slot = lax.broadcasted_iota(jnp.int32, shape, 0)
    mine = jnp.where(slot < tok, place[0] * tok + slot, place[1] * tok + slot - tok)
    token = lax.broadcasted_iota(jnp.int32, shape, 1)
    numbers = jnp.broadcast_to(counts[...].astype(F32), shape)
    kinds = jnp.broadcast_to(types[...].astype(F32), shape)

    def total(wanted, values):
        return jnp.sum(jnp.where(wanted, values, 0.0), axis=1, keepdims=True)

    columns = [
        total(token < mine, numbers),
        total(token <= mine, numbers),
        total(token == mine, numbers),
        total(token == mine, kinds),
    ]
    kind = lax.broadcasted_iota(jnp.int32, (2 * tok, w_restype.shape[0]), 1)
    picked = jnp.where(kind == columns[3].astype(jnp.int32), 1.0, 0.0).astype(BF16)
    embedded[...] = nn(picked, w_restype[...])
    lane = lax.broadcasted_iota(jnp.int32, tokens.shape, 1)
    table = jnp.zeros(tokens.shape, F32)
    for n, column in enumerate(columns):
        table = jnp.where(lane == n, column, table)
    tokens[...] = table.astype(jnp.int32)
    every = lax.broadcasted_iota(jnp.int32, counts.shape, 1)
    for k in range(2):
        first = place[k] * tok
        start = jnp.sum(jnp.where(every < first, counts[...], 0))
        end = jnp.sum(jnp.where(every < first + tok, counts[...], 0))
        bounds[2 * k] = start // chunk
        bounds[2 * k + 1] = (end + chunk - 1) // chunk
    bounds[4] = place[0] % 2
    for g in range(tok // 8):
        chosen[g] = choice(g, tok, False)
    move.wait()


def turned_rows(g, source, tok):
    rows = [source[pl.ds(g * 8 + n, tok, stride=tok), :] for n in range(8)]
    return jnp.concatenate(rows, axis=0)


def turn_kernel(d_pair, out, wide, made, sem):
    tok = d_pair.shape[0]
    span = 8 * tok
    wide[...] = d_pair[...].astype(F32).reshape(wide.shape)

    def grads(g, carry):
        rows = pl.ds(pl.multiple_of(g * span, span), span)
        made[rows, :] = turned_rows(g, wide, tok).astype(BF16)
        return carry

    lax.fori_loop(0, tok // 8, grads, 0)
    move = pltpu.make_async_copy(made, out, sem)
    move.start()
    move.wait()


def choice(g, tok, turned):
    shape = (2 * tok, 8 * tok)
    source = lax.broadcasted_iota(jnp.int32, shape, 0)
    token = lax.broadcasted_iota(jnp.int32, shape, 1)
    high, low = g * 8 + token // tok, token % tok
    left, right = (low, high) if turned else (high, low)
    wanted = (source == left) | (source == right + tok)
    return jnp.where(wanted, 1.0, 0.0).astype(BF16)


def front_kernel(bounds, same, other, tokens, embedded, w_atom, w_pair, plain, chosen, mask, gain, weights, send, sides, wide, feats, pair_in, sem):
    groups, width, span = plain.shape
    tok = span // 8
    devices = send.shape[0]
    move = pltpu.make_async_copy(plain, pair_in, sem)
    move.start()
    chunks, chunk = feats.shape[0], feats.shape[1]
    for n in range(chunks // 2):
        feats[2 * n + bounds[4]] = same[n * chunk : (n + 1) * chunk, :]
        feats[2 * n + 1 - bounds[4]] = other[n * chunk : (n + 1) * chunk, :]

    def pool(n, sums):
        out = []
        for k in range(2):
            q = bounds[2 * k] + n
            act = jnp.maximum(nn(feats[jnp.minimum(q, chunks - 1)], w_atom[...]), 0.0).astype(BF16)
            atoms = lax.broadcasted_iota(jnp.int32, (tok, chunk), 1) + q * chunk
            starts = tokens[k * tok : (k + 1) * tok, 0:1]
            ends = tokens[k * tok : (k + 1) * tok, 1:2]
            mine = (atoms >= starts) & (atoms < ends)
            out.append(sums[k] + nn(jnp.where(mine, 1.0, 0.0).astype(BF16), act))
        return tuple(out)

    steps = jnp.maximum(bounds[1] - bounds[0], bounds[3] - bounds[2])
    zero = jnp.zeros((tok, w_atom.shape[1]), F32)
    sums = lax.fori_loop(0, steps, pool, (zero, zero))
    counts = tokens[:, 2:3].astype(F32)
    single = (jnp.concatenate(sums, 0) / counts + embedded[...]).astype(BF16)
    left = nn(single[:tok], w_pair[:, :width])
    right = nn(single[tok:], w_pair[:, width:])
    sides[...] = jnp.concatenate([left, right], 0).T.astype(BF16)
    move.wait()

    for g in range(0, groups, FRONT):
        block = beside(pair_in, g, FRONT).astype(F32) + nn(sides[...], beside(chosen, g, FRONT))
        normed = norm(block.astype(BF16).astype(F32), widened(gain, FRONT), 0).astype(BF16)
        send_groups(g, normed, weights[...], mask, wide, devices)
    send[...] = wide[...].astype(BF16).reshape(send.shape)


def first_gate_kernel(pair_in, sides, gain, w_gate, pair_out, gate_out, wide, pair, gate, sems):
    tok = pair_in.shape[0]
    wide[...] = pair_in[...].astype(F32).reshape(wide.shape)

    def group(g, carry):
        block = turned_rows(g, wide, tok).T + nn(sides[...], choice(g, tok, True))
        block = block.astype(BF16)
        pair[g] = block
        normed = norm(block.astype(F32), gain[...], 0).astype(BF16)
        gate[g] = sigmoid(nn(w_gate[...], normed)).astype(BF16)
        return carry

    lax.fori_loop(0, tok // 8, group, 0)
    moves = [
        pltpu.make_async_copy(pair, pair_out, sems.at[0]),
        pltpu.make_async_copy(gate, gate_out, sems.at[1]),
    ]
    for move in moves:
        move.start()
    for move in moves:
        move.wait()


def windows_of(parts, tok, start):
    lane = lax.broadcasted_iota(jnp.int32, parts[0].shape, 1)
    out = []
    for w in range(len(parts) * LANES // tok):
        q, off = divmod(w * tok, LANES)
        turn = (start - off) % LANES
        value = parts[q] if turn == 0 else pltpu.roll(parts[q], turn, 1)
        if off + tok > LANES:
            rest = parts[q + 1] if turn == 0 else pltpu.roll(parts[q + 1], turn, 1)
            value = jnp.where(lane < start + LANES - off, value, rest)
        out.append(value)
    return out


def triangle_kernel(tok, blocks, x, out, xf, lhs, rhs, moved, of, made, sems):
    devices = x.shape[0]
    share = out.shape[1] * LANES // (tok * tok)
    parts = 3
    each = out.shape[1]
    groups = tok // 8
    kinds = 2 * share
    side_len = blocks * tok
    xf[...] = x[...].astype(F32).reshape(xf.shape)
    lane = lax.broadcasted_iota(jnp.int32, (tok, LANES), 1)
    per_block = devices // blocks * x.shape[1]

    half = LANES // 2
    used = lane % half < tok
    for b in range(0, blocks, 2):
        cols = slice(b * half, b * half + LANES)
        for kind in range(kinds):
            side, e = divmod(kind, share)
            pairs = []
            for n in range(2):
                tiles = [
                    xf[pl.ds((b + n) * per_block + kind * parts + q, tok, stride=kinds * parts), :]
                    for q in range(parts)
                ]
                pairs.append(windows_of(tiles, tok, n * half))
            for w in range(8):
                value = jnp.where(lane < half, pairs[0][w], pairs[1][w])
                rows = slice(w * tok, (w + 1) * tok)
                if side == 0:
                    rhs[e, rows, cols] = jnp.where(used, value, 0.0).astype(BF16)
                else:
                    lhs[e, rows, cols] = value.astype(BF16)

    width = blocks * half
    source = lax.broadcasted_iota(jnp.int32, (side_len, width), 0)
    target = lax.broadcasted_iota(jnp.int32, (side_len, width), 1)
    block, spot = target // half, target % half
    wanted = (spot % 8) * tok + block * groups + spot // 8
    place = jnp.where((source == wanted) & (spot < tok), 1.0, 0.0).astype(BF16)
    for e in range(share):
        product = nt(lhs[e], rhs[e]).astype(BF16)
        moved[e] = nn(product, place)

    leaving = []
    for b in range(blocks):
        at, start = b // 2 * LANES, b % 2 * half
        for e in range(share):
            tiles = [None] * parts
            for w in range(8):
                value = moved[e, w * tok : (w + 1) * tok, at : at + LANES]
                q, off = divmod(w * tok, LANES)
                turn = (off - start) % LANES
                first = value if turn == 0 else pltpu.roll(value, turn, 1)
                tiles[q] = first if tiles[q] is None else jnp.where(lane >= off, first, tiles[q])
                if off + tok > LANES:
                    tiles[q + 1] = first
            for q in range(parts):
                base = b * blocks * out.shape[1] + e * parts + q
                of[pl.ds(base, tok, stride=share * parts), :] = tiles[q]
        if made is None:
            continue
        here = pl.ds(b * blocks, blocks)
        rows = slice(b * blocks * each, (b + 1) * blocks * each)
        made[here] = of[rows].astype(BF16).reshape(blocks, each, LANES)
        leaving.append(pltpu.make_async_copy(made.at[here], out.at[here], sems.at[b]))
        leaving[-1].start()
    for copy in leaving:
        copy.wait()
    if made is None:
        out[...] = of[...].astype(BF16).reshape(out.shape)


def updated_groups(first, each, devices, wide, gain, w_out, pair, gate):
    parts = 3
    share = w_out.shape[1] // devices
    tiles = [
        jnp.concatenate(
            [
                wide[pl.ds((g * share + e) * parts + q, devices, stride=each), :]
                for g in range(first, first + LATE)
                for q in range(parts)
            ],
            axis=1,
        )
        for e in range(share)
    ]
    normed = norm(jnp.concatenate(tiles, axis=0), widened(gain, LATE), 0).astype(BF16)
    change = beside(gate, first, LATE).astype(F32) * nn(w_out[...], normed)
    return (beside(pair, first, LATE).astype(F32) + change).astype(BF16)


def middle_kernel(tri, pair, gate, gain_out, w_out, mask, gain, weights, w_gate, send, pair_new, gate_new, thin, wide, here, gates, sems):
    devices, each = tri.shape[0], tri.shape[1]
    groups = pair.shape[0]
    moves = [
        (
            pltpu.make_async_copy(pair.at[g], here.at[g], sems.at[0, g]),
            pltpu.make_async_copy(gate.at[g], gates.at[g], sems.at[1, g]),
        )
        for g in range(groups)
    ]
    for both in moves:
        for move in both:
            move.start()
    thin[...] = tri[...].astype(F32).reshape(thin.shape)
    for g in range(0, groups, LATE):
        for both in moves[g : g + LATE]:
            for move in both:
                move.wait()
        block = updated_groups(g, each, devices, thin, gain_out, w_out, here, gates)
        apart(pair_new, g, block)
        normed = norm(block.astype(F32), widened(gain, LATE), 0).astype(BF16)
        send_groups(g, normed, weights[...], mask, wide, devices)
        apart(gate_new, g, sigmoid(nn(w_gate[...], normed)).astype(BF16))
    send[...] = wide[...].astype(BF16).reshape(send.shape)


def last_kernel(tri, pair, gate, gain_out, w_out, gain, w_up, d_pair, grad, hidden, pair_new, thin, total, there, units, pairs, small, sems, outs):
    devices, each = tri.shape[0], tri.shape[1]
    groups, span = pair.shape[0], pair.shape[2]
    move = pltpu.make_async_copy(d_pair, there, sems.at[0])
    move.start()
    thin[...] = tri[...].astype(F32).reshape(thin.shape)
    expand = total.shape[0]
    leaving = []
    for g in range(0, groups, LATE):
        block = updated_groups(g, each, devices, thin, gain_out, w_out, pair, gate)
        apart(pairs, g, block)
        normed = norm(block.astype(F32), widened(gain, LATE), 0).astype(BF16)
        up = nn(w_up[...], normed)
        first = up[:expand]
        made = (first * sigmoid(first) * up[expand:]).astype(BF16)
        apart(units, g, made)
        for n in range(g, g + LATE):
            for copy in (
                pltpu.make_async_copy(pairs.at[n], pair_new.at[n], outs.at[0, n]),
                pltpu.make_async_copy(units.at[n], hidden.at[n], outs.at[1, n]),
            ):
                copy.start()
                leaving.append(copy)
        if g == 0:
            move.wait()
        part = nn(made, there[g * span : (g + LATE) * span, :])
        total[...] = part if g == 0 else total[...] + part
    small[...] = total[...].astype(BF16)
    leaving.append(pltpu.make_async_copy(small, grad, sems.at[1]))
    leaving[-1].start()
    for copy in leaving:
        copy.wait()


def down_kernel(hidden, pair, w_down, out, wide):
    tok = out.shape[0]

    def group(g, carry):
        result = (pair[g].astype(F32) + nn(w_down[...], hidden[g])).T
        for n in range(8):
            wide[pl.ds(g * 8 + n, tok, stride=tok), :] = result[n * tok : (n + 1) * tok]
        return carry

    lax.fori_loop(0, hidden.shape[0], group, 0)
    out[...] = wide[...].astype(BF16).reshape(out.shape)


def call(kernel, outs, scratch, name, cost, *args, far=(), far_out=(), scalar=(), scalar_out=()):
    space = [
        pltpu.SMEM if n in scalar else pltpu.HBM if n in far else pltpu.VMEM for n in range(len(args))
    ]
    args = [
        pltpu.with_memory_space_constraint(arg, pltpu.HBM) if n in far else arg
        for n, arg in enumerate(args)
    ]
    many = isinstance(outs, tuple)
    out_space = [
        pltpu.HBM if n in far_out else pltpu.SMEM if n in scalar_out else pltpu.VMEM for n in range(len(outs) if many else 1)
    ]
    out_specs = tuple(pl.BlockSpec(memory_space=s) for s in out_space)
    listed = [
        pltpu.HBM(o.shape, o.dtype) if n in far_out else o
        for n, o in enumerate(outs if many else (outs,))
    ]
    outs = tuple(listed) if many else listed[0]
    return pl.pallas_call(
        kernel,
        out_shape=outs,
        in_specs=[pl.BlockSpec(memory_space=s) for s in space],
        out_specs=out_specs if many else out_specs[0],
        scratch_shapes=scratch,
        compiler_params=PARAMS,
        name=name,
        cost_estimate=pl.CostEstimate(flops=cost, bytes_accessed=4 * 2**20, transcendentals=10**6),
    )(*args)


def local(
    atom_feats,
    atom_token,
    atom_counts,
    restype,
    pair_in,
    pair_mask,
    w_atom,
    w_restype,
    w_pair,
    ln_tri,
    w_tri_in,
    ln_tri_out,
    w_tri_out,
    ln_trans,
    w_up,
    w_down,
    d_pair,
):
    n_row, n_col = lax.axis_size(ROW), lax.axis_size(COL)
    devices = n_row * n_col
    tok = pair_in.shape[1]
    width = pair_in.shape[3]
    inner = w_tri_out.shape[1]
    expand = w_down.shape[0]
    share = inner // devices
    count = tok * tok
    groups = tok // 8
    span = 8 * tok

    shape = jax.ShapeDtypeStruct
    cost = 400 * 10**6
    half = devices // 2
    spread = jnp.broadcast_to(atom_feats, (half,) + atom_feats.shape[1:])
    same = exchange(spread, ("x", "y", "zl")).reshape(-1, atom_feats.shape[-1])

    plain, tokens, bounds, chosen, embedded = call(
        functools.partial(prepare_kernel, n_col * atom_feats.shape[1]),
        (
            shape((groups, width, span), BF16),
            shape((2 * tok, 4), jnp.int32),
            shape((5,), jnp.int32),
            shape((groups, 2 * tok, span), BF16),
            shape((2 * tok, w_restype.shape[1]), F32),
        ),
        [
            pltpu.VMEM((count, width), F32),
            pltpu.VMEM((groups, width, span), BF16),
            pltpu.SemaphoreType.DMA,
        ],
        "prepare",
        cost,
        jnp.stack([lax.axis_index(ROW), lax.axis_index(COL)]).astype(jnp.int32),
        pair_in[0],
        atom_counts,
        restype,
        w_restype,
        far_out=(0,),
        scalar=(0,),
        scalar_out=(2,),
    )
    same, bounds = lax.optimization_barrier((same, bounds))
    other = lax.ppermute(same, "core", [(0, 1), (1, 0)])
    valid = pair_mask[0].astype(F32)
    mask = valid.reshape(groups, span)

    def column(gain):
        return jnp.broadcast_to(gain[:, None], (gain.shape[0], span))

    def side_weights(weights):
        blocks = weights[:, : 4 * inner].reshape(width, 2, 2, devices, share)
        return blocks.transpose(2, 1, 4, 3, 0).reshape(4 * inner, width)

    def by_owner(values, update):
        if update == 0:
            order = values.reshape((n_col, n_row, share) + values.shape[1:]).swapaxes(0, 1)
        else:
            order = values.reshape((n_row, n_col, share) + values.shape[1:])
        return jnp.moveaxis(order, 2, 0).reshape(values.shape)

    rows_out = 2 * share * count // LANES
    rows_back = share * count // LANES
    send_shape = shape((devices, rows_out, LANES), BF16)
    back_shape = shape((devices, rows_back, LANES), BF16)
    wide = pltpu.VMEM((devices * rows_out, LANES), F32)
    thin = pltpu.VMEM((devices * rows_back, LANES), F32)
    flat = shape((groups, width, span), BF16)
    here = pltpu.VMEM(flat.shape, BF16)
    gates = here

    def triangle(value, leaves):
        blocks = n_row
        kernel = functools.partial(triangle_kernel, tok, blocks)
        if not leaves:
            kernel = lambda *refs: triangle_kernel(tok, blocks, *refs, None, None)
        extra = [pltpu.VMEM(back_shape.shape, BF16), pltpu.SemaphoreType.DMA((blocks,))]
        return call(
            kernel,
            back_shape,
            [
                wide,
                pltpu.VMEM((share, blocks * tok, blocks * LANES // 2), BF16),
                pltpu.VMEM((share, blocks * tok, blocks * LANES // 2), BF16),
                pltpu.VMEM((share, blocks * tok, blocks * LANES // 2), F32),
                thin,
                *(extra if leaves else []),
            ],
            "triangle",
            cost,
            value,
            far_out=(0,) if leaves else (),
        )

    send, sides = call(
        front_kernel,
        (send_shape, shape((width, 2 * tok), BF16)),
        [wide, pltpu.VMEM((n_row, n_col * atom_feats.shape[1], atom_feats.shape[2]), BF16), here, pltpu.SemaphoreType.DMA],
        "front",
        cost,
        bounds,
        same,
        other,
        tokens,
        embedded,
        w_atom,
        w_pair,
        plain,
        chosen,
        mask,
        column(ln_tri[0]),
        side_weights(w_tri_in[0]),
        far=(7,),
        scalar=(0,),
    )
    arrived = exchange(send, COL + ROW)
    arrived, sides, pair_in, d_pair, valid, w_tri_in, w_tri_out, ln_tri, ln_tri_out, w_up, w_down, ln_trans = (
        lax.optimization_barrier(
            (arrived, sides, pair_in, d_pair, valid, w_tri_in, w_tri_out, ln_tri, ln_tri_out, w_up, w_down, ln_trans)
        )
    )
    tri = exchange(triangle(arrived, True), ROW + COL)
    w_gates = w_tri_in[:, :, 4 * inner :].swapaxes(1, 2)
    w_outs = [by_owner(w_tri_out[u], u).T for u in range(2)]
    gains_out = [column(by_owner(ln_tri_out[u], u)) for u in range(2)]
    pair, gate = call(
        first_gate_kernel,
        (flat, flat),
        [pltpu.VMEM((count, width), F32), here, gates, pltpu.SemaphoreType.DMA((2,))],
        "first_gate",
        cost,
        pair_in[0],
        sides,
        column(ln_tri[0]),
        w_gates[0],
        far_out=(0, 1),
    )
    turned_grad = call(
        turn_kernel,
        shape((count, width), BF16),
        [pltpu.VMEM((count, width), F32), pltpu.VMEM((count, width), BF16), pltpu.SemaphoreType.DMA],
        "turn",
        cost,
        d_pair[0],
        far_out=(0,),
    )
    late = [gains_out[1], w_outs[1], column(ln_trans), w_up.T, w_down.T, turned_grad]
    ready = [
        gains_out[0],
        w_outs[0],
        valid.T.reshape(groups, span),
        column(ln_tri[1]),
        side_weights(w_tri_in[1]),
        w_gates[1],
    ]
    ready, late = lax.optimization_barrier((ready, late))
    send, pair, gate = call(
        middle_kernel,
        (send_shape, flat, flat),
        [thin, wide, here, gates, pltpu.SemaphoreType.DMA((2, groups))],
        "middle",
        cost,
        tri,
        pair,
        gate,
        *ready,
        far=(1, 2),
    )
    arrived = exchange(send, ROW + COL)
    tri = exchange(triangle(arrived, False), ROW + COL)
    grad, hidden, pair = call(
        last_kernel,
        (shape((expand, width), BF16), shape((groups, expand, span), BF16), flat),
        [
            thin,
            pltpu.VMEM((expand, width), F32),
            pltpu.VMEM((count, width), BF16),
            pltpu.VMEM((groups, expand, span), BF16),
            here,
            pltpu.VMEM((expand, width), BF16),
            pltpu.SemaphoreType.DMA((2,)),
            pltpu.SemaphoreType.DMA((2, groups)),
        ],
        "last",
        2 * cost,
        tri,
        pair,
        gate,
        late[0],
        late[1],
        late[2],
        late[3],
        late[5],
        far=(7,),
        far_out=(0, 1, 2),
    )
    everyone = devices * lax.axis_size("rep")
    grad = exchange(grad.reshape(everyone, expand // everyone, width), ROW + COL + ("rep",))
    result = call(
        down_kernel,
        shape((tok, tok, width), BF16),
        [pltpu.VMEM((count, width), F32)],
        "down",
        cost,
        hidden,
        pair,
        late[4],
    )
    return (result[None], jnp.sum(grad.astype(F32), axis=0))


def solution(mesh):
    rows, cols, reps = (mesh.shape[name] for name in ("row", "col", "rep"))
    parts = Mesh(
        mesh.devices.reshape(rows // 2, 2, cols // 2, 2, reps), ROW + COL + ("rep",)
    )
    pair = P("rep", ROW, COL, None)
    return jax.shard_map(
        local,
        mesh=parts,
        in_specs=(
            P("rep", ROW + COL, None),
            P("rep", ROW + COL),
            P("rep", None),
            P("rep", None),
            pair,
            P("rep", ROW, COL),
            *[P()] * 10,
            pair,
        ),
        out_specs=(pair, P(ROW + COL + ("rep",), None)),
        check_vma=False,
    )
```

```python
import functools

import jax
import jax.numpy as jnp
from jax import lax
from jax.experimental import pallas as pl
from jax.experimental.pallas import tpu as pltpu
from jax.sharding import Mesh, PartitionSpec as P

F32, BF16 = jnp.float32, jnp.bfloat16
LANES = 128
ROW, COL = ("x", "core"), ("y", "zl")
FRONT, LATE = 6, 3
PARAMS = pltpu.CompilerParams(vmem_limit_bytes=32 * 2**20)


def nt(a, b):
    return lax.dot_general(a, b, (((1,), (1,)), ((), ())), preferred_element_type=F32)


def nn(a, b):
    return lax.dot_general(a, b, (((1,), (0,)), ((), ())), preferred_element_type=F32)


def norm(values, scales, axis):
    average = jnp.mean(values, axis=axis, keepdims=True)
    centred = values - average
    variance = jnp.mean(centred * centred, axis=axis, keepdims=True)
    return centred * lax.rsqrt(variance + 1e-05) * scales


def sigmoid(x):
    return jax.nn.sigmoid(x)


def exchange(value, axes):
    return lax.all_to_all(value, axes, 0, 0, tiled=True)


def send_groups(first, normed, weights, mask, wide, devices):
    proj = nn(weights, normed)
    half = proj.shape[0] // 2
    span = mask.shape[1]
    count = proj.shape[1] // span
    valid = jnp.concatenate([mask[pl.ds(first + n, 1), :] for n in range(count)], axis=1)
    sides = sigmoid(proj[:half]) * proj[half:] * valid
    rows = wide.shape[0] // devices
    parts = span // LANES
    kinds = half // devices
    for n in range(count):
        for kind in range(kinds):
            for q in range(parts):
                at = n * span + q * LANES
                wide[pl.ds(((first + n) * kinds + kind) * parts + q, devices, stride=rows), :] = sides[
                    kind * devices : (kind + 1) * devices, at : at + LANES
                ]


def beside(array, first, count):
    return jnp.concatenate([array[first + n] for n in range(count)], axis=1)


def widened(gain, count):
    return jnp.concatenate([gain[...]] * count, axis=1)


def apart(array, first, value):
    span = array.shape[2]
    for n in range(value.shape[1] // span):
        array[first + n] = value[:, n * span : (n + 1) * span]


def prepare_kernel(chunk, place, pair_in, counts, types, w_restype, plain, tokens, bounds, chosen, embedded, wide, made, sem):
    tok, width = pair_in.shape[0], pair_in.shape[2]
    span = 8 * tok
    wide[...] = pair_in[...].astype(F32).reshape(wide.shape)

    def turn(g, carry):
        rows = pl.ds(pl.multiple_of(g * span, span), span)
        made[g] = wide[rows, :].T.astype(BF16)
        return carry

    lax.fori_loop(0, tok // 8, turn, 0)
    move = pltpu.make_async_copy(made, plain, sem)
    move.start()
    shape = (2 * tok, counts.shape[1])
    slot = lax.broadcasted_iota(jnp.int32, shape, 0)
    mine = jnp.where(slot < tok, place[0] * tok + slot, place[1] * tok + slot - tok)
    token = lax.broadcasted_iota(jnp.int32, shape, 1)
    numbers = jnp.broadcast_to(counts[...].astype(F32), shape)
    kinds = jnp.broadcast_to(types[...].astype(F32), shape)

    def total(wanted, values):
        return jnp.sum(jnp.where(wanted, values, 0.0), axis=1, keepdims=True)

    columns = [
        total(token < mine, numbers),
        total(token <= mine, numbers),
        total(token == mine, numbers),
        total(token == mine, kinds),
    ]
    kind = lax.broadcasted_iota(jnp.int32, (2 * tok, w_restype.shape[0]), 1)
    picked = jnp.where(kind == columns[3].astype(jnp.int32), 1.0, 0.0).astype(BF16)
    embedded[...] = nn(picked, w_restype[...])
    lane = lax.broadcasted_iota(jnp.int32, tokens.shape, 1)
    table = jnp.zeros(tokens.shape, F32)
    for n, column in enumerate(columns):
        table = jnp.where(lane == n, column, table)
    tokens[...] = table.astype(jnp.int32)
    every = lax.broadcasted_iota(jnp.int32, counts.shape, 1)
    for k in range(2):
        first = place[k] * tok
        start = jnp.sum(jnp.where(every < first, counts[...], 0))
        end = jnp.sum(jnp.where(every < first + tok, counts[...], 0))
        bounds[2 * k] = start // chunk
        bounds[2 * k + 1] = (end + chunk - 1) // chunk
    bounds[4] = place[0] % 2
    for g in range(tok // 8):
        chosen[g] = choice(g, tok, False)
    move.wait()


def turned_rows(g, source, tok):
    rows = [source[pl.ds(g * 8 + n, tok, stride=tok), :] for n in range(8)]
    return jnp.concatenate(rows, axis=0)


def turn_kernel(d_pair, out, wide, made, sem):
    tok = d_pair.shape[0]
    span = 8 * tok
    wide[...] = d_pair[...].astype(F32).reshape(wide.shape)

    def grads(g, carry):
        rows = pl.ds(pl.multiple_of(g * span, span), span)
        made[rows, :] = turned_rows(g, wide, tok).astype(BF16)
        return carry

    lax.fori_loop(0, tok // 8, grads, 0)
    move = pltpu.make_async_copy(made, out, sem)
    move.start()
    move.wait()


def choice(g, tok, turned):
    shape = (2 * tok, 8 * tok)
    source = lax.broadcasted_iota(jnp.int32, shape, 0)
    token = lax.broadcasted_iota(jnp.int32, shape, 1)
    high, low = g * 8 + token // tok, token % tok
    left, right = (low, high) if turned else (high, low)
    wanted = (source == left) | (source == right + tok)
    return jnp.where(wanted, 1.0, 0.0).astype(BF16)


def front_kernel(bounds, same, other, tokens, embedded, w_atom, w_pair, plain, chosen, mask, gain, weights, send, sides, wide, feats, pair_in, sem):
    groups, width, span = plain.shape
    tok = span // 8
    devices = send.shape[0]
    move = pltpu.make_async_copy(plain, pair_in, sem)
    move.start()
    chunks, chunk = feats.shape[0], feats.shape[1]
    for n in range(chunks // 2):
        feats[2 * n + bounds[4]] = same[n * chunk : (n + 1) * chunk, :]
        feats[2 * n + 1 - bounds[4]] = other[n * chunk : (n + 1) * chunk, :]

    def pool(n, sums):
        out = []
        for k in range(2):
            q = bounds[2 * k] + n
            act = jnp.maximum(nn(feats[jnp.minimum(q, chunks - 1)], w_atom[...]), 0.0).astype(BF16)
            atoms = lax.broadcasted_iota(jnp.int32, (tok, chunk), 1) + q * chunk
            starts = tokens[k * tok : (k + 1) * tok, 0:1]
            ends = tokens[k * tok : (k + 1) * tok, 1:2]
            mine = (atoms >= starts) & (atoms < ends)
            out.append(sums[k] + nn(jnp.where(mine, 1.0, 0.0).astype(BF16), act))
        return tuple(out)

    steps = jnp.maximum(bounds[1] - bounds[0], bounds[3] - bounds[2])
    zero = jnp.zeros((tok, w_atom.shape[1]), F32)
    sums = lax.fori_loop(0, steps, pool, (zero, zero))
    counts = tokens[:, 2:3].astype(F32)
    single = (jnp.concatenate(sums, 0) / counts + embedded[...]).astype(BF16)
    left = nn(single[:tok], w_pair[:, :width])
    right = nn(single[tok:], w_pair[:, width:])
    sides[...] = jnp.concatenate([left, right], 0).T.astype(BF16)
    move.wait()

    for g in range(0, groups, FRONT):
        block = beside(pair_in, g, FRONT).astype(F32) + nn(sides[...], beside(chosen, g, FRONT))
        normed = norm(block.astype(BF16).astype(F32), widened(gain, FRONT), 0).astype(BF16)
        send_groups(g, normed, weights[...], mask, wide, devices)
    send[...] = wide[...].astype(BF16).reshape(send.shape)


def first_gate_kernel(pair_in, sides, gain, w_gate, pair_out, gate_out, wide, pair, gate, sems):
    tok = pair_in.shape[0]
    wide[...] = pair_in[...].astype(F32).reshape(wide.shape)

    def group(g, carry):
        block = turned_rows(g, wide, tok).T + nn(sides[...], choice(g, tok, True))
        block = block.astype(BF16)
        pair[g] = block
        normed = norm(block.astype(F32), gain[...], 0).astype(BF16)
        gate[g] = sigmoid(nn(w_gate[...], normed)).astype(BF16)
        return carry

    lax.fori_loop(0, tok // 8, group, 0)
    moves = [
        pltpu.make_async_copy(pair, pair_out, sems.at[0]),
        pltpu.make_async_copy(gate, gate_out, sems.at[1]),
    ]
    for move in moves:
        move.start()
    for move in moves:
        move.wait()


def windows_of(parts, tok, start):
    lane = lax.broadcasted_iota(jnp.int32, parts[0].shape, 1)
    out = []
    for w in range(len(parts) * LANES // tok):
        q, off = divmod(w * tok, LANES)
        turn = (start - off) % LANES
        value = parts[q] if turn == 0 else pltpu.roll(parts[q], turn, 1)
        if off + tok > LANES:
            rest = parts[q + 1] if turn == 0 else pltpu.roll(parts[q + 1], turn, 1)
            value = jnp.where(lane < start + LANES - off, value, rest)
        out.append(value)
    return out


def triangle_kernel(tok, blocks, x, out, xf, lhs, rhs, moved, of, made, sems):
    devices = x.shape[0]
    share = out.shape[1] * LANES // (tok * tok)
    parts = 3
    each = out.shape[1]
    groups = tok // 8
    kinds = 2 * share
    side_len = blocks * tok
    xf[...] = x[...].astype(F32).reshape(xf.shape)
    lane = lax.broadcasted_iota(jnp.int32, (tok, LANES), 1)
    per_block = devices // blocks * x.shape[1]

    half = LANES // 2
    used = lane % half < tok
    for b in range(0, blocks, 2):
        cols = slice(b * half, b * half + LANES)
        for kind in range(kinds):
            side, e = divmod(kind, share)
            pairs = []
            for n in range(2):
                tiles = [
                    xf[pl.ds((b + n) * per_block + kind * parts + q, tok, stride=kinds * parts), :]
                    for q in range(parts)
                ]
                pairs.append(windows_of(tiles, tok, n * half))
            for w in range(8):
                value = jnp.where(lane < half, pairs[0][w], pairs[1][w])
                rows = slice(w * tok, (w + 1) * tok)
                if side == 0:
                    rhs[e, rows, cols] = jnp.where(used, value, 0.0).astype(BF16)
                else:
                    lhs[e, rows, cols] = value.astype(BF16)

    width = blocks * half
    source = lax.broadcasted_iota(jnp.int32, (side_len, width), 0)
    target = lax.broadcasted_iota(jnp.int32, (side_len, width), 1)
    block, spot = target // half, target % half
    wanted = (spot % 8) * tok + block * groups + spot // 8
    place = jnp.where((source == wanted) & (spot < tok), 1.0, 0.0).astype(BF16)
    products = [nt(lhs[e], rhs[e]).astype(BF16) for e in range(share)]
    leaving = []
    for b in range(blocks):
        if b % (blocks // 2) == 0:
            some = slice(b * half, (b + blocks // 2) * half)
            for e in range(share):
                moved[e, :, some] = nn(products[e], place[:, some])
        at, start = b // 2 * LANES, b % 2 * half
        for e in range(share):
            tiles = [None] * parts
            for w in range(8):
                value = moved[e, w * tok : (w + 1) * tok, at : at + LANES]
                q, off = divmod(w * tok, LANES)
                turn = (off - start) % LANES
                first = value if turn == 0 else pltpu.roll(value, turn, 1)
                tiles[q] = first if tiles[q] is None else jnp.where(lane >= off, first, tiles[q])
                if off + tok > LANES:
                    tiles[q + 1] = first
            for q in range(parts):
                base = b * blocks * out.shape[1] + e * parts + q
                of[pl.ds(base, tok, stride=share * parts), :] = tiles[q]
        if made is None:
            continue
        here = pl.ds(b * blocks, blocks)
        rows = slice(b * blocks * each, (b + 1) * blocks * each)
        made[here] = of[rows].astype(BF16).reshape(blocks, each, LANES)
        leaving.append(pltpu.make_async_copy(made.at[here], out.at[here], sems.at[b]))
        leaving[-1].start()
    for copy in leaving:
        copy.wait()
    if made is None:
        out[...] = of[...].astype(BF16).reshape(out.shape)


def change_of(first, each, devices, wide, gain, w_out):
    parts = 3
    share = w_out.shape[1] // devices
    tiles = [
        jnp.concatenate(
            [
                wide[pl.ds((g * share + e) * parts + q, devices, stride=each), :]
                for g in range(first, first + LATE)
                for q in range(parts)
            ],
            axis=1,
        )
        for e in range(share)
    ]
    normed = norm(jnp.concatenate(tiles, axis=0), widened(gain, LATE), 0).astype(BF16)
    return nn(w_out[...], normed)


def updated(first, change, pair, gate):
    gated = beside(gate, first, LATE).astype(F32) * change
    return (beside(pair, first, LATE).astype(F32) + gated).astype(BF16)


def middle_kernel(tri, pair, gate, gain_out, w_out, mask, gain, weights, w_gate, send, pair_new, gate_new, thin, wide, here, gates, sems):
    devices, each = tri.shape[0], tri.shape[1]
    groups = pair.shape[0]
    moves = [
        (
            pltpu.make_async_copy(pair.at[g], here.at[g], sems.at[0, g]),
            pltpu.make_async_copy(gate.at[g], gates.at[g], sems.at[1, g]),
        )
        for g in range(groups)
    ]
    for both in moves:
        for move in both:
            move.start()
    thin[...] = tri[...].astype(F32).reshape(thin.shape)
    changes = [
        change_of(g, each, devices, thin, gain_out, w_out) for g in range(0, groups, LATE)
    ]
    for g in range(0, groups, LATE):
        for both in moves[g : g + LATE]:
            for move in both:
                move.wait()
        block = updated(g, changes[g // LATE], here, gates)
        apart(pair_new, g, block)
        normed = norm(block.astype(F32), widened(gain, LATE), 0).astype(BF16)
        send_groups(g, normed, weights[...], mask, wide, devices)
        apart(gate_new, g, sigmoid(nn(w_gate[...], normed)).astype(BF16))
    send[...] = wide[...].astype(BF16).reshape(send.shape)


def last_kernel(tri, pair, gate, gain_out, w_out, gain, w_up, d_pair, grad, hidden, pair_new, thin, total, there, units, pairs, small, sems, outs):
    devices, each = tri.shape[0], tri.shape[1]
    groups, span = pair.shape[0], pair.shape[2]
    move = pltpu.make_async_copy(d_pair, there, sems.at[0])
    move.start()
    thin[...] = tri[...].astype(F32).reshape(thin.shape)
    expand = total.shape[0]
    leaving = []
    for g in range(0, groups, LATE):
        change = change_of(g, each, devices, thin, gain_out, w_out)
        block = updated(g, change, pair, gate)
        apart(pairs, g, block)
        normed = norm(block.astype(F32), widened(gain, LATE), 0).astype(BF16)
        lanes = []
        for at in range(0, normed.shape[1], span):
            some, pieces = normed[:, at : at + span], []
            for f in range(0, expand, LANES):
                first = nn(w_up[f : f + LANES, :], some)
                second = nn(w_up[expand + f : expand + f + LANES, :], some)
                pieces.append((first * sigmoid(first) * second).astype(BF16))
            lanes.append(jnp.concatenate(pieces, axis=0))
        made = jnp.concatenate(lanes, axis=1)
        apart(units, g, made)
        for n in range(g, g + LATE):
            for copy in (
                pltpu.make_async_copy(pairs.at[n], pair_new.at[n], outs.at[0, n]),
                pltpu.make_async_copy(units.at[n], hidden.at[n], outs.at[1, n]),
            ):
                copy.start()
                leaving.append(copy)
        if g == 0:
            move.wait()
        part = nn(made, there[g * span : (g + LATE) * span, :])
        total[...] = part if g == 0 else total[...] + part
    small[...] = total[...].astype(BF16)
    leaving.append(pltpu.make_async_copy(small, grad, sems.at[1]))
    leaving[-1].start()
    for copy in leaving:
        copy.wait()


def down_kernel(hidden, pair, w_down, out, wide):
    tok = out.shape[0]

    def group(g, carry):
        result = (pair[g].astype(F32) + nn(w_down[...], hidden[g])).T
        for n in range(8):
            wide[pl.ds(g * 8 + n, tok, stride=tok), :] = result[n * tok : (n + 1) * tok]
        return carry

    lax.fori_loop(0, hidden.shape[0], group, 0)
    out[...] = wide[...].astype(BF16).reshape(out.shape)


def call(kernel, outs, scratch, name, cost, *args, far=(), far_out=(), scalar=(), scalar_out=()):
    space = [
        pltpu.SMEM if n in scalar else pltpu.HBM if n in far else pltpu.VMEM for n in range(len(args))
    ]
    args = [
        pltpu.with_memory_space_constraint(arg, pltpu.HBM) if n in far else arg
        for n, arg in enumerate(args)
    ]
    many = isinstance(outs, tuple)
    out_space = [
        pltpu.HBM if n in far_out else pltpu.SMEM if n in scalar_out else pltpu.VMEM for n in range(len(outs) if many else 1)
    ]
    out_specs = tuple(pl.BlockSpec(memory_space=s) for s in out_space)
    listed = [
        pltpu.HBM(o.shape, o.dtype) if n in far_out else o
        for n, o in enumerate(outs if many else (outs,))
    ]
    outs = tuple(listed) if many else listed[0]
    return pl.pallas_call(
        kernel,
        out_shape=outs,
        in_specs=[pl.BlockSpec(memory_space=s) for s in space],
        out_specs=out_specs if many else out_specs[0],
        scratch_shapes=scratch,
        compiler_params=PARAMS,
        name=name,
        cost_estimate=pl.CostEstimate(flops=cost, bytes_accessed=4 * 2**20, transcendentals=10**6),
    )(*args)


def local(
    atom_feats,
    atom_token,
    atom_counts,
    restype,
    pair_in,
    pair_mask,
    w_atom,
    w_restype,
    w_pair,
    ln_tri,
    w_tri_in,
    ln_tri_out,
    w_tri_out,
    ln_trans,
    w_up,
    w_down,
    d_pair,
):
    n_row, n_col = lax.axis_size(ROW), lax.axis_size(COL)
    devices = n_row * n_col
    tok = pair_in.shape[1]
    width = pair_in.shape[3]
    inner = w_tri_out.shape[1]
    expand = w_down.shape[0]
    share = inner // devices
    count = tok * tok
    groups = tok // 8
    span = 8 * tok

    shape = jax.ShapeDtypeStruct
    cost = 400 * 10**6
    half = devices // 2
    spread = jnp.broadcast_to(atom_feats, (half,) + atom_feats.shape[1:])
    same = exchange(spread, ("x", "y", "zl")).reshape(-1, atom_feats.shape[-1])

    plain, tokens, bounds, chosen, embedded = call(
        functools.partial(prepare_kernel, n_col * atom_feats.shape[1]),
        (
            shape((groups, width, span), BF16),
            shape((2 * tok, 4), jnp.int32),
            shape((5,), jnp.int32),
            shape((groups, 2 * tok, span), BF16),
            shape((2 * tok, w_restype.shape[1]), F32),
        ),
        [
            pltpu.VMEM((count, width), F32),
            pltpu.VMEM((groups, width, span), BF16),
            pltpu.SemaphoreType.DMA,
        ],
        "prepare",
        cost,
        jnp.stack([lax.axis_index(ROW), lax.axis_index(COL)]).astype(jnp.int32),
        pair_in[0],
        atom_counts,
        restype,
        w_restype,
        far_out=(0,),
        scalar=(0,),
        scalar_out=(2,),
    )
    same, bounds = lax.optimization_barrier((same, bounds))
    other = lax.ppermute(same, "core", [(0, 1), (1, 0)])
    valid = pair_mask[0].astype(F32)
    mask = valid.reshape(groups, span)

    def column(gain):
        return jnp.broadcast_to(gain[:, None], (gain.shape[0], span))

    def side_weights(weights):
        blocks = weights[:, : 4 * inner].reshape(width, 2, 2, devices, share)
        return blocks.transpose(2, 1, 4, 3, 0).reshape(4 * inner, width)

    def by_owner(values, update):
        if update == 0:
            order = values.reshape((n_col, n_row, share) + values.shape[1:]).swapaxes(0, 1)
        else:
            order = values.reshape((n_row, n_col, share) + values.shape[1:])
        return jnp.moveaxis(order, 2, 0).reshape(values.shape)

    rows_out = 2 * share * count // LANES
    rows_back = share * count // LANES
    send_shape = shape((devices, rows_out, LANES), BF16)
    back_shape = shape((devices, rows_back, LANES), BF16)
    wide = pltpu.VMEM((devices * rows_out, LANES), F32)
    thin = pltpu.VMEM((devices * rows_back, LANES), F32)
    flat = shape((groups, width, span), BF16)
    here = pltpu.VMEM(flat.shape, BF16)
    gates = here

    def triangle(value, leaves):
        blocks = n_row
        kernel = functools.partial(triangle_kernel, tok, blocks)
        if not leaves:
            kernel = lambda *refs: triangle_kernel(tok, blocks, *refs, None, None)
        extra = [pltpu.VMEM(back_shape.shape, BF16), pltpu.SemaphoreType.DMA((blocks,))]
        return call(
            kernel,
            back_shape,
            [
                wide,
                pltpu.VMEM((share, blocks * tok, blocks * LANES // 2), BF16),
                pltpu.VMEM((share, blocks * tok, blocks * LANES // 2), BF16),
                pltpu.VMEM((share, blocks * tok, blocks * LANES // 2), F32),
                thin,
                *(extra if leaves else []),
            ],
            "triangle",
            cost,
            value,
            far_out=(0,) if leaves else (),
        )

    send, sides = call(
        front_kernel,
        (send_shape, shape((width, 2 * tok), BF16)),
        [wide, pltpu.VMEM((n_row, n_col * atom_feats.shape[1], atom_feats.shape[2]), BF16), here, pltpu.SemaphoreType.DMA],
        "front",
        cost,
        bounds,
        same,
        other,
        tokens,
        embedded,
        w_atom,
        w_pair,
        plain,
        chosen,
        mask,
        column(ln_tri[0]),
        side_weights(w_tri_in[0]),
        far=(7,),
        scalar=(0,),
    )
    arrived = exchange(send, COL + ROW)
    arrived, sides, pair_in, d_pair, valid, w_tri_in, w_tri_out, ln_tri, ln_tri_out, w_up, w_down, ln_trans = (
        lax.optimization_barrier(
            (arrived, sides, pair_in, d_pair, valid, w_tri_in, w_tri_out, ln_tri, ln_tri_out, w_up, w_down, ln_trans)
        )
    )
    tri = exchange(triangle(arrived, True), ROW + COL)
    w_gates = w_tri_in[:, :, 4 * inner :].swapaxes(1, 2)
    w_outs = [by_owner(w_tri_out[u], u).T for u in range(2)]
    gains_out = [column(by_owner(ln_tri_out[u], u)) for u in range(2)]
    pair, gate = call(
        first_gate_kernel,
        (flat, flat),
        [pltpu.VMEM((count, width), F32), here, gates, pltpu.SemaphoreType.DMA((2,))],
        "first_gate",
        cost,
        pair_in[0],
        sides,
        column(ln_tri[0]),
        w_gates[0],
        far_out=(0, 1),
    )
    turned_grad = call(
        turn_kernel,
        shape((count, width), BF16),
        [pltpu.VMEM((count, width), F32), pltpu.VMEM((count, width), BF16), pltpu.SemaphoreType.DMA],
        "turn",
        cost,
        d_pair[0],
        far_out=(0,),
    )
    late = [gains_out[1], w_outs[1], column(ln_trans), w_up.T, w_down.T, turned_grad]
    ready = [
        gains_out[0],
        w_outs[0],
        valid.T.reshape(groups, span),
        column(ln_tri[1]),
        side_weights(w_tri_in[1]),
        w_gates[1],
    ]
    ready, late = lax.optimization_barrier((ready, late))
    send, pair, gate = call(
        middle_kernel,
        (send_shape, flat, flat),
        [thin, wide, here, gates, pltpu.SemaphoreType.DMA((2, groups))],
        "middle",
        cost,
        tri,
        pair,
        gate,
        *ready,
        far=(1, 2),
    )
    arrived = exchange(send, ROW + COL)
    tri = exchange(triangle(arrived, False), ROW + COL)
    grad, hidden, pair = call(
        last_kernel,
        (shape((expand, width), BF16), shape((groups, expand, span), BF16), flat),
        [
            thin,
            pltpu.VMEM((expand, width), F32),
            pltpu.VMEM((count, width), BF16),
            pltpu.VMEM((groups, expand, span), BF16),
            here,
            pltpu.VMEM((expand, width), BF16),
            pltpu.SemaphoreType.DMA((2,)),
            pltpu.SemaphoreType.DMA((2, groups)),
        ],
        "last",
        2 * cost,
        tri,
        pair,
        gate,
        late[0],
        late[1],
        late[2],
        late[3],
        late[5],
        far=(7,),
        far_out=(0, 1, 2),
    )
    everyone = devices * lax.axis_size("rep")
    grad = exchange(grad.reshape(everyone, expand // everyone, width), ROW + COL + ("rep",))
    result = call(
        down_kernel,
        shape((tok, tok, width), BF16),
        [pltpu.VMEM((count, width), F32)],
        "down",
        cost,
        hidden,
        pair,
        late[4],
    )
    return (result[None], jnp.sum(grad.astype(F32), axis=0))


def solution(mesh):
    rows, cols, reps = (mesh.shape[name] for name in ("row", "col", "rep"))
    parts = Mesh(
        mesh.devices.reshape(rows // 2, 2, cols // 2, 2, reps), ROW + COL + ("rep",)
    )
    pair = P("rep", ROW, COL, None)
    return jax.shard_map(
        local,
        mesh=parts,
        in_specs=(
            P("rep", ROW + COL, None),
            P("rep", ROW + COL),
            P("rep", None),
            P("rep", None),
            pair,
            P("rep", ROW, COL),
            *[P()] * 10,
            pair,
        ),
        out_specs=(pair, P(ROW + COL + ("rep",), None)),
        check_vma=False,
    )
```

```python
import functools

import jax
import jax.numpy as jnp
from jax import lax
from jax.experimental import pallas as pl
from jax.experimental.pallas import tpu as pltpu
from jax.sharding import Mesh, PartitionSpec as P

F32, BF16 = jnp.float32, jnp.bfloat16
LANES = 128
ROW, COL = ("x", "core"), ("y", "zl")
FRONT, LATE = 6, 3
PARAMS = pltpu.CompilerParams(vmem_limit_bytes=32 * 2**20)


def nt(a, b):
    return lax.dot_general(a, b, (((1,), (1,)), ((), ())), preferred_element_type=F32)


def nn(a, b):
    return lax.dot_general(a, b, (((1,), (0,)), ((), ())), preferred_element_type=F32)


def norm(values, scales, axis):
    average = jnp.mean(values, axis=axis, keepdims=True)
    centred = values - average
    variance = jnp.mean(centred * centred, axis=axis, keepdims=True)
    return centred * lax.rsqrt(variance + 1e-05) * scales


def sigmoid(x):
    return jax.nn.sigmoid(x)


def exchange(value, axes):
    return lax.all_to_all(value, axes, 0, 0, tiled=True)


def send_groups(first, normed, weights, mask, wide, devices):
    proj = nn(weights, normed)
    half = proj.shape[0] // 2
    span = mask.shape[1]
    count = proj.shape[1] // span
    valid = jnp.concatenate([mask[pl.ds(first + n, 1), :] for n in range(count)], axis=1)
    sides = sigmoid(proj[:half]) * proj[half:] * valid
    rows = wide.shape[0] // (devices + 1)
    parts = span // LANES
    kinds = half // devices
    for n in range(count):
        for kind in range(kinds):
            for q in range(parts):
                at = n * span + q * LANES
                wide[pl.ds(((first + n) * kinds + kind) * parts + q, devices, stride=rows), :] = sides[
                    kind * devices : (kind + 1) * devices, at : at + LANES
                ]


def beside(array, first, count):
    return jnp.concatenate([array[first + n] for n in range(count)], axis=1)


def widened(gain, count):
    return jnp.concatenate([gain[...]] * count, axis=1)


def apart(array, first, value):
    span = array.shape[2]
    for n in range(value.shape[1] // span):
        array[first + n] = value[:, n * span : (n + 1) * span]


def prepare_kernel(chunk, place, pair_in, counts, types, w_restype, plain, tokens, bounds, chosen, embedded, wide, made, sem):
    tok, width = pair_in.shape[0], pair_in.shape[2]
    span = 8 * tok
    wide[...] = pair_in[...].astype(F32).reshape(wide.shape)

    def turn(g, carry):
        rows = pl.ds(pl.multiple_of(g * span, span), span)
        made[g] = wide[rows, :].T.astype(BF16)
        return carry

    lax.fori_loop(0, tok // 8, turn, 0)
    move = pltpu.make_async_copy(made, plain, sem)
    move.start()
    shape = (2 * tok, counts.shape[1])
    slot = lax.broadcasted_iota(jnp.int32, shape, 0)
    mine = jnp.where(slot < tok, place[0] * tok + slot, place[1] * tok + slot - tok)
    token = lax.broadcasted_iota(jnp.int32, shape, 1)
    numbers = jnp.broadcast_to(counts[...].astype(F32), shape)
    kinds = jnp.broadcast_to(types[...].astype(F32), shape)

    def total(wanted, values):
        return jnp.sum(jnp.where(wanted, values, 0.0), axis=1, keepdims=True)

    columns = [
        total(token < mine, numbers),
        total(token <= mine, numbers),
        total(token == mine, numbers),
        total(token == mine, kinds),
    ]
    kind = lax.broadcasted_iota(jnp.int32, (2 * tok, w_restype.shape[0]), 1)
    picked = jnp.where(kind == columns[3].astype(jnp.int32), 1.0, 0.0).astype(BF16)
    embedded[...] = nn(picked, w_restype[...])
    lane = lax.broadcasted_iota(jnp.int32, tokens.shape, 1)
    table = jnp.zeros(tokens.shape, F32)
    for n, column in enumerate(columns):
        table = jnp.where(lane == n, column, table)
    tokens[...] = table.astype(jnp.int32)
    every = lax.broadcasted_iota(jnp.int32, counts.shape, 1)
    for k in range(2):
        first = place[k] * tok
        start = jnp.sum(jnp.where(every < first, counts[...], 0))
        end = jnp.sum(jnp.where(every < first + tok, counts[...], 0))
        bounds[2 * k] = start // chunk
        bounds[2 * k + 1] = (end + chunk - 1) // chunk
    bounds[4] = place[0] % 2
    for g in range(tok // 8):
        chosen[g] = choice(g, tok, False)
    move.wait()


def turned_rows(g, source, tok):
    rows = [source[pl.ds(g * 8 + n, tok, stride=tok), :] for n in range(8)]
    return jnp.concatenate(rows, axis=0)


def turn_kernel(d_pair, out, wide, made, sem):
    tok = d_pair.shape[0]
    span = 8 * tok
    wide[: tok * tok] = d_pair[...].astype(F32).reshape(tok * tok, d_pair.shape[2])

    def grads(g, carry):
        rows = pl.ds(pl.multiple_of(g * span, span), span)
        made[rows, :] = turned_rows(g, wide, tok).astype(BF16)
        return carry

    lax.fori_loop(0, tok // 8, grads, 0)
    move = pltpu.make_async_copy(made, out, sem)
    move.start()
    move.wait()


def choice(g, tok, turned):
    shape = (2 * tok, 8 * tok)
    source = lax.broadcasted_iota(jnp.int32, shape, 0)
    token = lax.broadcasted_iota(jnp.int32, shape, 1)
    high, low = g * 8 + token // tok, token % tok
    left, right = (low, high) if turned else (high, low)
    wanted = (source == left) | (source == right + tok)
    return jnp.where(wanted, 1.0, 0.0).astype(BF16)


def front_kernel(bounds, same, other, tokens, embedded, w_atom, w_pair, plain, chosen, mask, gain, weights, send, sides, wide, feats, pair_in, sem):
    groups, width, span = plain.shape
    tok = span // 8
    devices = send.shape[0]
    move = pltpu.make_async_copy(plain, pair_in, sem)
    move.start()
    chunks, chunk = feats.shape[0], feats.shape[1]
    for n in range(chunks // 2):
        feats[2 * n + bounds[4]] = same[n * chunk : (n + 1) * chunk, :]
        feats[2 * n + 1 - bounds[4]] = other[n * chunk : (n + 1) * chunk, :]

    def pool(n, sums):
        out = []
        for k in range(2):
            q = bounds[2 * k] + n
            act = jnp.maximum(nn(feats[jnp.minimum(q, chunks - 1)], w_atom[...]), 0.0).astype(BF16)
            atoms = lax.broadcasted_iota(jnp.int32, (tok, chunk), 1) + q * chunk
            starts = tokens[k * tok : (k + 1) * tok, 0:1]
            ends = tokens[k * tok : (k + 1) * tok, 1:2]
            mine = (atoms >= starts) & (atoms < ends)
            out.append(sums[k] + nn(jnp.where(mine, 1.0, 0.0).astype(BF16), act))
        return tuple(out)

    steps = jnp.maximum(bounds[1] - bounds[0], bounds[3] - bounds[2])
    zero = jnp.zeros((tok, w_atom.shape[1]), F32)
    sums = pool(1, pool(0, (zero, zero)))
    sums = lax.fori_loop(2, jnp.maximum(steps, 2), pool, sums)
    counts = tokens[:, 2:3].astype(F32)
    single = (jnp.concatenate(sums, 0) / counts + embedded[...]).astype(BF16)
    left = nn(single[:tok], w_pair[:, :width])
    right = nn(single[tok:], w_pair[:, width:])
    sides[...] = jnp.concatenate([left, right], 0).T.astype(BF16)
    move.wait()

    for g in range(0, groups, FRONT):
        block = beside(pair_in, g, FRONT).astype(F32) + nn(sides[...], beside(chosen, g, FRONT))
        normed = norm(block.astype(BF16).astype(F32), widened(gain, FRONT), 0).astype(BF16)
        send_groups(g, normed, weights[...], mask, wide, devices)
    send[...] = wide[: devices * send.shape[1]].astype(BF16).reshape(send.shape)


def first_gate_kernel(pair_in, sides, gain, w_gate, pair_out, gate_out, wide, pair, gate, sems):
    tok = pair_in.shape[0]
    wide[: tok * tok] = pair_in[...].astype(F32).reshape(tok * tok, pair_in.shape[2])

    def group(g, carry):
        block = turned_rows(g, wide, tok).T + nn(sides[...], choice(g, tok, True))
        block = block.astype(BF16)
        pair[g] = block
        normed = norm(block.astype(F32), gain[...], 0).astype(BF16)
        gate[g] = sigmoid(nn(w_gate[...], normed)).astype(BF16)
        return carry

    lax.fori_loop(0, tok // 8, group, 0)
    moves = [
        pltpu.make_async_copy(pair, pair_out, sems.at[0]),
        pltpu.make_async_copy(gate, gate_out, sems.at[1]),
    ]
    for move in moves:
        move.start()
    for move in moves:
        move.wait()


def windows_of(parts, tok, start):
    lane = lax.broadcasted_iota(jnp.int32, parts[0].shape, 1)
    out = []
    for w in range(len(parts) * LANES // tok):
        q, off = divmod(w * tok, LANES)
        turn = (start - off) % LANES
        value = parts[q] if turn == 0 else pltpu.roll(parts[q], turn, 1)
        if off + tok > LANES:
            rest = parts[q + 1] if turn == 0 else pltpu.roll(parts[q + 1], turn, 1)
            value = jnp.where(lane < start + LANES - off, value, rest)
        out.append(value)
    return out


def triangle_kernel(tok, blocks, x, out, xf, lhs, rhs, moved, of, made, sems):
    devices = x.shape[0]
    share = out.shape[1] * LANES // (tok * tok)
    parts = 3
    each = out.shape[1]
    groups = tok // 8
    kinds = 2 * share
    side_len = blocks * tok
    xf[: devices * x.shape[1]] = x[...].astype(F32).reshape(devices * x.shape[1], LANES)
    lane = lax.broadcasted_iota(jnp.int32, (tok, LANES), 1)
    per_block = devices // blocks * x.shape[1]

    half = LANES // 2
    used = lane % half < tok
    for b in range(0, blocks, 2):
        cols = slice(b * half, b * half + LANES)
        for kind in range(kinds):
            side, e = divmod(kind, share)
            pairs = []
            for n in range(2):
                tiles = [
                    xf[pl.ds((b + n) * per_block + kind * parts + q, tok, stride=kinds * parts), :]
                    for q in range(parts)
                ]
                pairs.append(windows_of(tiles, tok, n * half))
            for w in range(8):
                value = jnp.where(lane < half, pairs[0][w], pairs[1][w])
                rows = slice(w * tok, (w + 1) * tok)
                if side == 0:
                    rhs[e, rows, cols] = jnp.where(used, value, 0.0).astype(BF16)
                else:
                    lhs[e, rows, cols] = value.astype(BF16)

    width = blocks * half
    source = lax.broadcasted_iota(jnp.int32, (side_len, width), 0)
    target = lax.broadcasted_iota(jnp.int32, (side_len, width), 1)
    block, spot = target // half, target % half
    wanted = (spot % 8) * tok + block * groups + spot // 8
    place = jnp.where((source == wanted) & (spot < tok), 1.0, 0.0).astype(BF16)
    products = [nt(lhs[e], rhs[e]).astype(BF16) for e in range(share)]
    leaving = []
    for b in range(blocks):
        if b % (blocks // 2) == 0:
            some = slice(b * half, (b + blocks // 2) * half)
            for e in range(share):
                moved[e, :, some] = nn(products[e], place[:, some])
        at, start = b // 2 * LANES, b % 2 * half
        for e in range(share):
            tiles = [None] * parts
            for w in range(8):
                value = moved[e, w * tok : (w + 1) * tok, at : at + LANES]
                q, off = divmod(w * tok, LANES)
                turn = (off - start) % LANES
                first = value if turn == 0 else pltpu.roll(value, turn, 1)
                tiles[q] = first if tiles[q] is None else jnp.where(lane >= off, first, tiles[q])
                if off + tok > LANES:
                    tiles[q + 1] = first
            for q in range(parts):
                base = b * blocks * out.shape[1] + e * parts + q
                of[pl.ds(base, tok, stride=share * parts), :] = tiles[q]
        if made is None:
            continue
        here = pl.ds(b * blocks, blocks)
        rows = slice(b * blocks * each, (b + 1) * blocks * each)
        made[here] = of[rows].astype(BF16).reshape(blocks, each, LANES)
        leaving.append(pltpu.make_async_copy(made.at[here], out.at[here], sems.at[b]))
        leaving[-1].start()
    for copy in leaving:
        copy.wait()
    if made is None:
        out[...] = of[: devices * each].astype(BF16).reshape(out.shape)


def change_of(first, each, devices, wide, gain, w_out):
    parts = 3
    share = w_out.shape[1] // devices
    tiles = [
        jnp.concatenate(
            [
                wide[pl.ds((g * share + e) * parts + q, devices, stride=each), :]
                for g in range(first, first + LATE)
                for q in range(parts)
            ],
            axis=1,
        )
        for e in range(share)
    ]
    normed = norm(jnp.concatenate(tiles, axis=0), widened(gain, LATE), 0).astype(BF16)
    return nn(w_out[...], normed)


def updated(first, change, pair, gate):
    gated = beside(gate, first, LATE).astype(F32) * change
    return (beside(pair, first, LATE).astype(F32) + gated).astype(BF16)


def middle_kernel(tri, pair, gate, gain_out, w_out, mask, gain, weights, w_gate, send, pair_new, gate_new, thin, wide, here, gates, sems):
    devices, each = tri.shape[0], tri.shape[1]
    groups = pair.shape[0]
    moves = [
        (
            pltpu.make_async_copy(pair.at[g], here.at[g], sems.at[0, g]),
            pltpu.make_async_copy(gate.at[g], gates.at[g], sems.at[1, g]),
        )
        for g in range(groups)
    ]
    for both in moves:
        for move in both:
            move.start()
    thin[: devices * each] = tri[...].astype(F32).reshape(devices * each, LANES)
    changes = [
        change_of(g, each, devices, thin, gain_out, w_out) for g in range(0, groups, LATE)
    ]
    for g in range(0, groups, LATE):
        for both in moves[g : g + LATE]:
            for move in both:
                move.wait()
        block = updated(g, changes[g // LATE], here, gates)
        apart(pair_new, g, block)
        normed = norm(block.astype(F32), widened(gain, LATE), 0).astype(BF16)
        send_groups(g, normed, weights[...], mask, wide, devices)
        apart(gate_new, g, sigmoid(nn(w_gate[...], normed)).astype(BF16))
    send[...] = wide[: devices * send.shape[1]].astype(BF16).reshape(send.shape)


def last_kernel(tri, pair, gate, gain_out, w_out, gain, w_up, d_pair, grad, hidden, pair_new, thin, total, there, units, pairs, small, sems, outs):
    devices, each = tri.shape[0], tri.shape[1]
    groups, span = pair.shape[0], pair.shape[2]
    move = pltpu.make_async_copy(d_pair, there, sems.at[0])
    move.start()
    thin[: devices * each] = tri[...].astype(F32).reshape(devices * each, LANES)
    expand = total.shape[0]
    leaving = []
    for g in range(0, groups, LATE):
        change = change_of(g, each, devices, thin, gain_out, w_out)
        block = updated(g, change, pair, gate)
        apart(pairs, g, block)
        normed = norm(block.astype(F32), widened(gain, LATE), 0).astype(BF16)
        lanes = []
        for at in range(0, normed.shape[1], span):
            some, pieces = normed[:, at : at + span], []
            for f in range(0, expand, LANES):
                first = nn(w_up[f : f + LANES, :], some)
                second = nn(w_up[expand + f : expand + f + LANES, :], some)
                pieces.append((first * sigmoid(first) * second).astype(BF16))
            lanes.append(jnp.concatenate(pieces, axis=0))
        made = jnp.concatenate(lanes, axis=1)
        apart(units, g, made)
        for n in range(g, g + LATE):
            for copy in (
                pltpu.make_async_copy(pairs.at[n], pair_new.at[n], outs.at[0, n]),
                pltpu.make_async_copy(units.at[n], hidden.at[n], outs.at[1, n]),
            ):
                copy.start()
                leaving.append(copy)
        if g == 0:
            move.wait()
        part = nn(made, there[g * span : (g + LATE) * span, :])
        total[...] = part if g == 0 else total[...] + part
    small[...] = total[...].astype(BF16)
    leaving.append(pltpu.make_async_copy(small, grad, sems.at[1]))
    leaving[-1].start()
    for copy in leaving:
        copy.wait()


def down_kernel(hidden, pair, w_down, out, wide):
    tok = out.shape[0]

    def group(g, carry):
        result = (pair[g].astype(F32) + nn(w_down[...], hidden[g])).T
        for n in range(8):
            wide[pl.ds(g * 8 + n, tok, stride=tok), :] = result[n * tok : (n + 1) * tok]
        return carry

    lax.fori_loop(0, hidden.shape[0], group, 0)
    out[...] = wide[: tok * tok].astype(BF16).reshape(out.shape)


def call(kernel, outs, scratch, name, cost, *args, far=(), far_out=(), scalar=(), scalar_out=()):
    space = [
        pltpu.SMEM if n in scalar else pltpu.HBM if n in far else pltpu.VMEM for n in range(len(args))
    ]
    args = [
        pltpu.with_memory_space_constraint(arg, pltpu.HBM) if n in far else arg
        for n, arg in enumerate(args)
    ]
    many = isinstance(outs, tuple)
    out_space = [
        pltpu.HBM if n in far_out else pltpu.SMEM if n in scalar_out else pltpu.VMEM for n in range(len(outs) if many else 1)
    ]
    out_specs = tuple(pl.BlockSpec(memory_space=s) for s in out_space)
    listed = [
        pltpu.HBM(o.shape, o.dtype) if n in far_out else o
        for n, o in enumerate(outs if many else (outs,))
    ]
    outs = tuple(listed) if many else listed[0]
    return pl.pallas_call(
        kernel,
        out_shape=outs,
        in_specs=[pl.BlockSpec(memory_space=s) for s in space],
        out_specs=out_specs if many else out_specs[0],
        scratch_shapes=scratch,
        compiler_params=PARAMS,
        name=name,
        cost_estimate=pl.CostEstimate(flops=cost, bytes_accessed=4 * 2**20, transcendentals=10**6),
    )(*args)


def local(
    atom_feats,
    atom_token,
    atom_counts,
    restype,
    pair_in,
    pair_mask,
    w_atom,
    w_restype,
    w_pair,
    ln_tri,
    w_tri_in,
    ln_tri_out,
    w_tri_out,
    ln_trans,
    w_up,
    w_down,
    d_pair,
):
    n_row, n_col = lax.axis_size(ROW), lax.axis_size(COL)
    devices = n_row * n_col
    tok = pair_in.shape[1]
    width = pair_in.shape[3]
    inner = w_tri_out.shape[1]
    expand = w_down.shape[0]
    share = inner // devices
    count = tok * tok
    groups = tok // 8
    span = 8 * tok

    shape = jax.ShapeDtypeStruct
    cost = 400 * 10**6
    half = devices // 2
    spread = jnp.broadcast_to(atom_feats, (half,) + atom_feats.shape[1:])
    same = exchange(spread, ("x", "y", "zl")).reshape(-1, atom_feats.shape[-1])

    plain, tokens, bounds, chosen, embedded = call(
        functools.partial(prepare_kernel, n_col * atom_feats.shape[1]),
        (
            shape((groups, width, span), BF16),
            shape((2 * tok, 4), jnp.int32),
            shape((5,), jnp.int32),
            shape((groups, 2 * tok, span), BF16),
            shape((2 * tok, w_restype.shape[1]), F32),
        ),
        [
            pltpu.VMEM((count, width), F32),
            pltpu.VMEM((groups, width, span), BF16),
            pltpu.SemaphoreType.DMA,
        ],
        "prepare",
        cost,
        jnp.stack([lax.axis_index(ROW), lax.axis_index(COL)]).astype(jnp.int32),
        pair_in[0],
        atom_counts,
        restype,
        w_restype,
        far_out=(0,),
        scalar=(0,),
        scalar_out=(2,),
    )
    same, bounds = lax.optimization_barrier((same, bounds))
    other = lax.ppermute(same, "core", [(0, 1), (1, 0)])
    valid = pair_mask[0].astype(F32)
    mask = valid.reshape(groups, span)

    def column(gain):
        return jnp.broadcast_to(gain[:, None], (gain.shape[0], span))

    def side_weights(weights):
        blocks = weights[:, : 4 * inner].reshape(width, 2, 2, devices, share)
        return blocks.transpose(2, 1, 4, 3, 0).reshape(4 * inner, width)

    def by_owner(values, update):
        if update == 0:
            order = values.reshape((n_col, n_row, share) + values.shape[1:]).swapaxes(0, 1)
        else:
            order = values.reshape((n_row, n_col, share) + values.shape[1:])
        return jnp.moveaxis(order, 2, 0).reshape(values.shape)

    rows_out = 2 * share * count // LANES
    rows_back = share * count // LANES
    send_shape = shape((devices, rows_out, LANES), BF16)
    back_shape = shape((devices, rows_back, LANES), BF16)
    wide = pltpu.VMEM(((devices + 1) * rows_out, LANES), F32)
    thin = pltpu.VMEM(((devices + 1) * rows_back, LANES), F32)
    strided = pltpu.VMEM((count + tok, width), F32)
    flat = shape((groups, width, span), BF16)
    here = pltpu.VMEM(flat.shape, BF16)
    gates = here

    def triangle(value, leaves):
        blocks = n_row
        kernel = functools.partial(triangle_kernel, tok, blocks)
        if not leaves:
            kernel = lambda *refs: triangle_kernel(tok, blocks, *refs, None, None)
        extra = [pltpu.VMEM(back_shape.shape, BF16), pltpu.SemaphoreType.DMA((blocks,))]
        return call(
            kernel,
            back_shape,
            [
                wide,
                pltpu.VMEM((share, blocks * tok, blocks * LANES // 2), BF16),
                pltpu.VMEM((share, blocks * tok, blocks * LANES // 2), BF16),
                pltpu.VMEM((share, blocks * tok, blocks * LANES // 2), F32),
                thin,
                *(extra if leaves else []),
            ],
            "triangle",
            cost,
            value,
            far_out=(0,) if leaves else (),
        )

    send, sides = call(
        front_kernel,
        (send_shape, shape((width, 2 * tok), BF16)),
        [wide, pltpu.VMEM((n_row, n_col * atom_feats.shape[1], atom_feats.shape[2]), BF16), here, pltpu.SemaphoreType.DMA],
        "front",
        cost,
        bounds,
        same,
        other,
        tokens,
        embedded,
        w_atom,
        w_pair,
        plain,
        chosen,
        mask,
        column(ln_tri[0]),
        side_weights(w_tri_in[0]),
        far=(7,),
        scalar=(0,),
    )
    arrived = exchange(send, COL + ROW)
    arrived, sides, pair_in, d_pair, valid, w_tri_in, w_tri_out, ln_tri, ln_tri_out, w_up, w_down, ln_trans = (
        lax.optimization_barrier(
            (arrived, sides, pair_in, d_pair, valid, w_tri_in, w_tri_out, ln_tri, ln_tri_out, w_up, w_down, ln_trans)
        )
    )
    tri = exchange(triangle(arrived, True), ROW + COL)
    w_gates = w_tri_in[:, :, 4 * inner :].swapaxes(1, 2)
    w_outs = [by_owner(w_tri_out[u], u).T for u in range(2)]
    gains_out = [column(by_owner(ln_tri_out[u], u)) for u in range(2)]
    pair, gate = call(
        first_gate_kernel,
        (flat, flat),
        [strided, here, gates, pltpu.SemaphoreType.DMA((2,))],
        "first_gate",
        cost,
        pair_in[0],
        sides,
        column(ln_tri[0]),
        w_gates[0],
        far_out=(0, 1),
    )
    turned_grad = call(
        turn_kernel,
        shape((count, width), BF16),
        [strided, pltpu.VMEM((count, width), BF16), pltpu.SemaphoreType.DMA],
        "turn",
        cost,
        d_pair[0],
        far_out=(0,),
    )
    late = [gains_out[1], w_outs[1], column(ln_trans), w_up.T, w_down.T, turned_grad]
    ready = [
        gains_out[0],
        w_outs[0],
        valid.T.reshape(groups, span),
        column(ln_tri[1]),
        side_weights(w_tri_in[1]),
        w_gates[1],
    ]
    ready, late = lax.optimization_barrier((ready, late))
    send, pair, gate = call(
        middle_kernel,
        (send_shape, flat, flat),
        [thin, wide, here, gates, pltpu.SemaphoreType.DMA((2, groups))],
        "middle",
        cost,
        tri,
        pair,
        gate,
        *ready,
        far=(1, 2),
    )
    arrived = exchange(send, ROW + COL)
    tri = exchange(triangle(arrived, False), ROW + COL)
    grad, hidden, pair = call(
        last_kernel,
        (shape((expand, width), BF16), shape((groups, expand, span), BF16), flat),
        [
            thin,
            pltpu.VMEM((expand, width), F32),
            pltpu.VMEM((count, width), BF16),
            pltpu.VMEM((groups, expand, span), BF16),
            here,
            pltpu.VMEM((expand, width), BF16),
            pltpu.SemaphoreType.DMA((2,)),
            pltpu.SemaphoreType.DMA((2, groups)),
        ],
        "last",
        2 * cost,
        tri,
        pair,
        gate,
        late[0],
        late[1],
        late[2],
        late[3],
        late[5],
        far=(7,),
        far_out=(0, 1, 2),
    )
    everyone = devices * lax.axis_size("rep")
    grad = exchange(grad.reshape(everyone, expand // everyone, width), ROW + COL + ("rep",))
    result = call(
        down_kernel,
        shape((tok, tok, width), BF16),
        [strided],
        "down",
        cost,
        hidden,
        pair,
        late[4],
    )
    return (result[None], jnp.sum(grad.astype(F32), axis=0))


def solution(mesh):
    rows, cols, reps = (mesh.shape[name] for name in ("row", "col", "rep"))
    parts = Mesh(
        mesh.devices.reshape(rows // 2, 2, cols // 2, 2, reps), ROW + COL + ("rep",)
    )
    pair = P("rep", ROW, COL, None)
    return jax.shard_map(
        local,
        mesh=parts,
        in_specs=(
            P("rep", ROW + COL, None),
            P("rep", ROW + COL),
            P("rep", None),
            P("rep", None),
            pair,
            P("rep", ROW, COL),
            *[P()] * 10,
            pair,
        ),
        out_specs=(pair, P(ROW + COL + ("rep",), None)),
        check_vma=False,
    )
```

```python
import functools

import jax
import jax.numpy as jnp
from jax import lax
from jax.experimental import pallas as pl
from jax.experimental.pallas import tpu as pltpu
from jax.sharding import Mesh, PartitionSpec as P

F32, BF16 = jnp.float32, jnp.bfloat16
LANES = 128
ROW, COL = ("x", "core"), ("y", "zl")
FRONT, LATE = 6, 3
PARAMS = pltpu.CompilerParams(vmem_limit_bytes=32 * 2**20)


def nt(a, b):
    return lax.dot_general(a, b, (((1,), (1,)), ((), ())), preferred_element_type=F32)


def nn(a, b):
    return lax.dot_general(a, b, (((1,), (0,)), ((), ())), preferred_element_type=F32)


def norm(values, scales, axis):
    average = jnp.mean(values, axis=axis, keepdims=True)
    centred = values - average
    variance = jnp.mean(centred * centred, axis=axis, keepdims=True)
    return centred * lax.rsqrt(variance + 1e-05) * scales


def sigmoid(x):
    return jax.nn.sigmoid(x)


def exchange(value, axes):
    return lax.all_to_all(value, axes, 0, 0, tiled=True)


def send_groups(first, normed, weights, mask, wide, devices):
    proj = nn(weights, normed)
    half = proj.shape[0] // 2
    span = mask.shape[1]
    count = proj.shape[1] // span
    valid = jnp.concatenate([mask[pl.ds(first + n, 1), :] for n in range(count)], axis=1)
    sides = sigmoid(proj[:half]) * proj[half:] * valid
    rows = wide.shape[0] // (devices + 1)
    parts = span // LANES
    kinds = half // devices
    for n in range(count):
        for kind in range(kinds):
            for q in range(parts):
                at = n * span + q * LANES
                wide[pl.ds(((first + n) * kinds + kind) * parts + q, devices, stride=rows), :] = sides[
                    kind * devices : (kind + 1) * devices, at : at + LANES
                ]


def beside(array, first, count):
    return jnp.concatenate([array[first + n] for n in range(count)], axis=1)


def widened(gain, count):
    return jnp.concatenate([gain[...]] * count, axis=1)


def apart(array, first, value):
    span = array.shape[2]
    for n in range(value.shape[1] // span):
        array[first + n] = value[:, n * span : (n + 1) * span]


def prepare_kernel(chunk, place, pair_in, counts, types, w_restype, plain, tokens, bounds, chosen, embedded, wide, made, sem):
    tok, width = pair_in.shape[0], pair_in.shape[2]
    span = 8 * tok
    wide[...] = pair_in[...].astype(F32).reshape(wide.shape)

    def turn(g, carry):
        rows = pl.ds(pl.multiple_of(g * span, span), span)
        made[g] = wide[rows, :].T.astype(BF16)
        return carry

    lax.fori_loop(0, tok // 8, turn, 0)
    move = pltpu.make_async_copy(made, plain, sem)
    move.start()
    shape = (2 * tok, counts.shape[1])
    slot = lax.broadcasted_iota(jnp.int32, shape, 0)
    mine = jnp.where(slot < tok, place[0] * tok + slot, place[1] * tok + slot - tok)
    token = lax.broadcasted_iota(jnp.int32, shape, 1)
    numbers = jnp.broadcast_to(counts[...].astype(F32), shape)
    kinds = jnp.broadcast_to(types[...].astype(F32), shape)

    def total(wanted, values):
        return jnp.sum(jnp.where(wanted, values, 0.0), axis=1, keepdims=True)

    columns = [
        total(token < mine, numbers),
        total(token <= mine, numbers),
        total(token == mine, numbers),
        total(token == mine, kinds),
    ]
    kind = lax.broadcasted_iota(jnp.int32, (2 * tok, w_restype.shape[0]), 1)
    picked = jnp.where(kind == columns[3].astype(jnp.int32), 1.0, 0.0).astype(BF16)
    embedded[...] = nn(picked, w_restype[...])
    lane = lax.broadcasted_iota(jnp.int32, tokens.shape, 1)
    table = jnp.zeros(tokens.shape, F32)
    for n, column in enumerate(columns):
        table = jnp.where(lane == n, column, table)
    tokens[...] = table.astype(jnp.int32)
    every = lax.broadcasted_iota(jnp.int32, counts.shape, 1)
    for k in range(2):
        first = place[k] * tok
        start = jnp.sum(jnp.where(every < first, counts[...], 0))
        end = jnp.sum(jnp.where(every < first + tok, counts[...], 0))
        bounds[2 * k] = start // chunk
        bounds[2 * k + 1] = (end + chunk - 1) // chunk
    bounds[4] = place[0] % 2
    for g in range(tok // 8):
        chosen[g] = choice(g, tok, False)
    move.wait()


def turned_rows(g, source, tok):
    rows = [source[pl.ds(g * 8 + n, tok, stride=tok), :] for n in range(8)]
    return jnp.concatenate(rows, axis=0)


def turn_kernel(d_pair, out, wide, made, sem):
    tok = d_pair.shape[0]
    span = 8 * tok
    wide[: tok * tok] = d_pair[...].astype(F32).reshape(tok * tok, d_pair.shape[2])

    def grads(g, carry):
        rows = pl.ds(pl.multiple_of(g * span, span), span)
        made[rows, :] = turned_rows(g, wide, tok).astype(BF16)
        return carry

    lax.fori_loop(0, tok // 8, grads, 0)
    move = pltpu.make_async_copy(made, out, sem)
    move.start()
    move.wait()


def choice(g, tok, turned):
    shape = (2 * tok, 8 * tok)
    source = lax.broadcasted_iota(jnp.int32, shape, 0)
    token = lax.broadcasted_iota(jnp.int32, shape, 1)
    high, low = g * 8 + token // tok, token % tok
    left, right = (low, high) if turned else (high, low)
    wanted = (source == left) | (source == right + tok)
    return jnp.where(wanted, 1.0, 0.0).astype(BF16)


def front_kernel(bounds, same, other, tokens, embedded, w_atom, w_pair, plain, chosen, mask, gain, weights, send, sides, wide, feats, pair_in, sem):
    groups, width, span = plain.shape
    tok = span // 8
    devices = send.shape[0]
    move = pltpu.make_async_copy(plain, pair_in, sem)
    move.start()
    chunks, chunk = feats.shape[0], feats.shape[1]
    for n in range(chunks // 2):
        feats[2 * n + bounds[4]] = same[n * chunk : (n + 1) * chunk, :]
        feats[2 * n + 1 - bounds[4]] = other[n * chunk : (n + 1) * chunk, :]

    def pool(n, sums):
        out = []
        for k in range(2):
            q = bounds[2 * k] + n
            act = jnp.maximum(nn(feats[jnp.minimum(q, chunks - 1)], w_atom[...]), 0.0).astype(BF16)
            atoms = lax.broadcasted_iota(jnp.int32, (tok, chunk), 1) + q * chunk
            starts = tokens[k * tok : (k + 1) * tok, 0:1]
            ends = tokens[k * tok : (k + 1) * tok, 1:2]
            mine = (atoms >= starts) & (atoms < ends)
            out.append(sums[k] + nn(jnp.where(mine, 1.0, 0.0).astype(BF16), act))
        return tuple(out)

    steps = jnp.maximum(bounds[1] - bounds[0], bounds[3] - bounds[2])
    zero = jnp.zeros((tok, w_atom.shape[1]), F32)
    sums = pool(1, pool(0, (zero, zero)))
    sums = lax.fori_loop(2, jnp.maximum(steps, 2), pool, sums)
    counts = tokens[:, 2:3].astype(F32)
    single = (jnp.concatenate(sums, 0) / counts + embedded[...]).astype(BF16)
    left = nn(single[:tok], w_pair[:, :width])
    right = nn(single[tok:], w_pair[:, width:])
    sides[...] = jnp.concatenate([left, right], 0).T.astype(BF16)
    move.wait()

    for g in range(0, groups, FRONT):
        block = beside(pair_in, g, FRONT).astype(F32) + nn(sides[...], beside(chosen, g, FRONT))
        normed = norm(block.astype(BF16).astype(F32), widened(gain, FRONT), 0).astype(BF16)
        send_groups(g, normed, weights[...], mask, wide, devices)
    send[...] = wide[: devices * send.shape[1]].astype(BF16).reshape(send.shape)


def first_gate_kernel(pair_in, sides, gain, w_gate, pair_out, gate_out, wide, pair, gate, sems):
    tok = pair_in.shape[0]
    wide[: tok * tok] = pair_in[...].astype(F32).reshape(tok * tok, pair_in.shape[2])

    def group(g, carry):
        block = turned_rows(g, wide, tok).T + nn(sides[...], choice(g, tok, True))
        block = block.astype(BF16)
        pair[g] = block
        normed = norm(block.astype(F32), gain[...], 0).astype(BF16)
        gate[g] = sigmoid(nn(w_gate[...], normed)).astype(BF16)
        return carry

    lax.fori_loop(0, tok // 8, group, 0)
    moves = [
        pltpu.make_async_copy(pair, pair_out, sems.at[0]),
        pltpu.make_async_copy(gate, gate_out, sems.at[1]),
    ]
    for move in moves:
        move.start()
    for move in moves:
        move.wait()


def windows_of(parts, tok, start):
    lane = lax.broadcasted_iota(jnp.int32, parts[0].shape, 1)
    out = []
    for w in range(len(parts) * LANES // tok):
        q, off = divmod(w * tok, LANES)
        turn = (start - off) % LANES
        value = parts[q] if turn == 0 else pltpu.roll(parts[q], turn, 1)
        if off + tok > LANES:
            rest = parts[q + 1] if turn == 0 else pltpu.roll(parts[q + 1], turn, 1)
            value = jnp.where(lane < start + LANES - off, value, rest)
        out.append(value)
    return out


def triangle_kernel(tok, blocks, x, out, xf, lhs, rhs, moved, of, made, sems):
    devices = x.shape[0]
    share = out.shape[1] * LANES // (tok * tok)
    parts = 3
    each = out.shape[1]
    groups = tok // 8
    kinds = 2 * share
    side_len = blocks * tok
    xf[: devices * x.shape[1]] = x[...].astype(F32).reshape(devices * x.shape[1], LANES)
    lane = lax.broadcasted_iota(jnp.int32, (tok, LANES), 1)
    per_block = devices // blocks * x.shape[1]

    half = LANES // 2
    used = lane % half < tok
    for b in range(0, blocks, 2):
        cols = slice(b * half, b * half + LANES)
        for kind in range(kinds):
            side, e = divmod(kind, share)
            pairs = []
            for n in range(2):
                tiles = [
                    xf[pl.ds((b + n) * per_block + kind * parts + q, tok, stride=kinds * parts), :]
                    for q in range(parts)
                ]
                pairs.append(windows_of(tiles, tok, n * half))
            for w in range(8):
                value = jnp.where(lane < half, pairs[0][w], pairs[1][w])
                rows = slice(w * tok, (w + 1) * tok)
                if side == 0:
                    rhs[e, rows, cols] = jnp.where(used, value, 0.0).astype(BF16)
                else:
                    lhs[e, rows, cols] = value.astype(BF16)

    width = blocks * half
    source = lax.broadcasted_iota(jnp.int32, (side_len, width), 0)
    target = lax.broadcasted_iota(jnp.int32, (side_len, width), 1)
    block, spot = target // half, target % half
    wanted = (spot % 8) * tok + block * groups + spot // 8
    place = jnp.where((source == wanted) & (spot < tok), 1.0, 0.0).astype(BF16)
    products = [nt(lhs[e], rhs[e]).astype(BF16) for e in range(share)]
    leaving = []
    for b in range(blocks):
        if b % (blocks // 2) == 0:
            some = slice(b * half, (b + blocks // 2) * half)
            for e in range(share):
                moved[e, :, some] = nn(products[e], place[:, some])
        at, start = b // 2 * LANES, b % 2 * half
        for e in range(share):
            tiles = [None] * parts
            for w in range(8):
                value = moved[e, w * tok : (w + 1) * tok, at : at + LANES]
                q, off = divmod(w * tok, LANES)
                turn = (off - start) % LANES
                first = value if turn == 0 else pltpu.roll(value, turn, 1)
                tiles[q] = first if tiles[q] is None else jnp.where(lane >= off, first, tiles[q])
                if off + tok > LANES:
                    tiles[q + 1] = first
            for q in range(parts):
                base = b * blocks * out.shape[1] + e * parts + q
                of[pl.ds(base, tok, stride=share * parts), :] = tiles[q]
        if made is None:
            continue
        here = pl.ds(b * blocks, blocks)
        rows = slice(b * blocks * each, (b + 1) * blocks * each)
        made[here] = of[rows].astype(BF16).reshape(blocks, each, LANES)
        leaving.append(pltpu.make_async_copy(made.at[here], out.at[here], sems.at[b]))
        leaving[-1].start()
    for copy in leaving:
        copy.wait()
    if made is None:
        out[...] = of[: devices * each].astype(BF16).reshape(out.shape)


def change_of(first, each, devices, wide, gain, w_out):
    parts = 3
    share = w_out.shape[1] // devices
    tiles = [
        jnp.concatenate(
            [
                wide[pl.ds((g * share + e) * parts + q, devices, stride=each), :]
                for g in range(first, first + LATE)
                for q in range(parts)
            ],
            axis=1,
        )
        for e in range(share)
    ]
    normed = norm(jnp.concatenate(tiles, axis=0), widened(gain, LATE), 0).astype(BF16)
    return nn(w_out[...], normed)


def updated(first, change, pair, gate):
    gated = beside(gate, first, LATE).astype(F32) * change
    return (beside(pair, first, LATE).astype(F32) + gated).astype(BF16)


def middle_kernel(tri, pair, gate, gain_out, w_out, mask, gain, weights, w_gate, send, pair_new, gate_new, thin, wide, here, gates, sems):
    devices, each = tri.shape[0], tri.shape[1]
    groups = pair.shape[0]
    moves = [
        (
            pltpu.make_async_copy(pair.at[g], here.at[g], sems.at[0, g]),
            pltpu.make_async_copy(gate.at[g], gates.at[g], sems.at[1, g]),
        )
        for g in range(groups)
    ]
    for both in moves:
        for move in both:
            move.start()
    thin[: devices * each] = tri[...].astype(F32).reshape(devices * each, LANES)
    for both in moves:
        for move in both:
            move.wait()
    changes = [
        change_of(g, each, devices, thin, gain_out, w_out) for g in range(0, groups, LATE)
    ]
    for g in range(0, groups, LATE):
        block = updated(g, changes[g // LATE], here, gates)
        apart(pair_new, g, block)
        normed = norm(block.astype(F32), widened(gain, LATE), 0).astype(BF16)
        send_groups(g, normed, weights[...], mask, wide, devices)
        apart(gate_new, g, sigmoid(nn(w_gate[...], normed)).astype(BF16))
    send[...] = wide[: devices * send.shape[1]].astype(BF16).reshape(send.shape)


def last_kernel(tri, pair, gate, gain_out, w_out, gain, w_up, d_pair, grad, hidden, pair_new, thin, total, there, units, pairs, small, sems, outs):
    devices, each = tri.shape[0], tri.shape[1]
    groups, span = pair.shape[0], pair.shape[2]
    move = pltpu.make_async_copy(d_pair, there, sems.at[0])
    move.start()
    thin[: devices * each] = tri[...].astype(F32).reshape(devices * each, LANES)
    expand = total.shape[0]
    leaving = []
    for g in range(0, groups, LATE):
        change = change_of(g, each, devices, thin, gain_out, w_out)
        block = updated(g, change, pair, gate)
        apart(pairs, g, block)
        normed = norm(block.astype(F32), widened(gain, LATE), 0).astype(BF16)
        lanes = []
        for at in range(0, normed.shape[1], span):
            some, pieces = normed[:, at : at + span], []
            for f in range(0, expand, LANES):
                first = nn(w_up[f : f + LANES, :], some)
                second = nn(w_up[expand + f : expand + f + LANES, :], some)
                pieces.append((first * sigmoid(first) * second).astype(BF16))
            lanes.append(jnp.concatenate(pieces, axis=0))
        made = jnp.concatenate(lanes, axis=1)
        apart(units, g, made)
        for n in range(g, g + LATE):
            for copy in (
                pltpu.make_async_copy(pairs.at[n], pair_new.at[n], outs.at[0, n]),
                pltpu.make_async_copy(units.at[n], hidden.at[n], outs.at[1, n]),
            ):
                copy.start()
                leaving.append(copy)
        if g == 0:
            move.wait()
        part = nn(made, there[g * span : (g + LATE) * span, :])
        total[...] = part if g == 0 else total[...] + part
    small[...] = total[...].astype(BF16)
    leaving.append(pltpu.make_async_copy(small, grad, sems.at[1]))
    leaving[-1].start()
    for copy in leaving:
        copy.wait()


def down_kernel(hidden, pair, w_down, out, wide):
    tok = out.shape[0]

    def group(g, carry):
        result = (pair[g].astype(F32) + nn(w_down[...], hidden[g])).T
        for n in range(8):
            wide[pl.ds(g * 8 + n, tok, stride=tok), :] = result[n * tok : (n + 1) * tok]
        return carry

    lax.fori_loop(0, hidden.shape[0], group, 0)
    out[...] = wide[: tok * tok].astype(BF16).reshape(out.shape)


def call(kernel, outs, scratch, name, cost, *args, far=(), far_out=(), scalar=(), scalar_out=()):
    space = [
        pltpu.SMEM if n in scalar else pltpu.HBM if n in far else pltpu.VMEM for n in range(len(args))
    ]
    args = [
        pltpu.with_memory_space_constraint(arg, pltpu.HBM) if n in far else arg
        for n, arg in enumerate(args)
    ]
    many = isinstance(outs, tuple)
    out_space = [
        pltpu.HBM if n in far_out else pltpu.SMEM if n in scalar_out else pltpu.VMEM for n in range(len(outs) if many else 1)
    ]
    out_specs = tuple(pl.BlockSpec(memory_space=s) for s in out_space)
    listed = [
        pltpu.HBM(o.shape, o.dtype) if n in far_out else o
        for n, o in enumerate(outs if many else (outs,))
    ]
    outs = tuple(listed) if many else listed[0]
    return pl.pallas_call(
        kernel,
        out_shape=outs,
        in_specs=[pl.BlockSpec(memory_space=s) for s in space],
        out_specs=out_specs if many else out_specs[0],
        scratch_shapes=scratch,
        compiler_params=PARAMS,
        name=name,
        cost_estimate=pl.CostEstimate(flops=cost, bytes_accessed=4 * 2**20, transcendentals=10**6),
    )(*args)


def local(
    atom_feats,
    atom_token,
    atom_counts,
    restype,
    pair_in,
    pair_mask,
    w_atom,
    w_restype,
    w_pair,
    ln_tri,
    w_tri_in,
    ln_tri_out,
    w_tri_out,
    ln_trans,
    w_up,
    w_down,
    d_pair,
):
    n_row, n_col = lax.axis_size(ROW), lax.axis_size(COL)
    devices = n_row * n_col
    tok = pair_in.shape[1]
    width = pair_in.shape[3]
    inner = w_tri_out.shape[1]
    expand = w_down.shape[0]
    share = inner // devices
    count = tok * tok
    groups = tok // 8
    span = 8 * tok

    shape = jax.ShapeDtypeStruct
    cost = 400 * 10**6
    half = devices // 2
    spread = jnp.broadcast_to(atom_feats, (half,) + atom_feats.shape[1:])
    same = exchange(spread, ("x", "y", "zl")).reshape(-1, atom_feats.shape[-1])

    plain, tokens, bounds, chosen, embedded = call(
        functools.partial(prepare_kernel, n_col * atom_feats.shape[1]),
        (
            shape((groups, width, span), BF16),
            shape((2 * tok, 4), jnp.int32),
            shape((5,), jnp.int32),
            shape((groups, 2 * tok, span), BF16),
            shape((2 * tok, w_restype.shape[1]), F32),
        ),
        [
            pltpu.VMEM((count, width), F32),
            pltpu.VMEM((groups, width, span), BF16),
            pltpu.SemaphoreType.DMA,
        ],
        "prepare",
        cost,
        jnp.stack([lax.axis_index(ROW), lax.axis_index(COL)]).astype(jnp.int32),
        pair_in[0],
        atom_counts,
        restype,
        w_restype,
        far_out=(0,),
        scalar=(0,),
        scalar_out=(2,),
    )
    same, bounds = lax.optimization_barrier((same, bounds))
    other = lax.ppermute(same, "core", [(0, 1), (1, 0)])
    valid = pair_mask[0].astype(F32)
    mask = valid.reshape(groups, span)

    def column(gain):
        return jnp.broadcast_to(gain[:, None], (gain.shape[0], span))

    def side_weights(weights):
        blocks = weights[:, : 4 * inner].reshape(width, 2, 2, devices, share)
        return blocks.transpose(2, 1, 4, 3, 0).reshape(4 * inner, width)

    def by_owner(values, update):
        if update == 0:
            order = values.reshape((n_col, n_row, share) + values.shape[1:]).swapaxes(0, 1)
        else:
            order = values.reshape((n_row, n_col, share) + values.shape[1:])
        return jnp.moveaxis(order, 2, 0).reshape(values.shape)

    rows_out = 2 * share * count // LANES
    rows_back = share * count // LANES
    send_shape = shape((devices, rows_out, LANES), BF16)
    back_shape = shape((devices, rows_back, LANES), BF16)
    wide = pltpu.VMEM(((devices + 1) * rows_out, LANES), F32)
    thin = pltpu.VMEM(((devices + 1) * rows_back, LANES), F32)
    strided = pltpu.VMEM((count + tok, width), F32)
    flat = shape((groups, width, span), BF16)
    here = pltpu.VMEM(flat.shape, BF16)
    gates = here

    def triangle(value, leaves):
        blocks = n_row
        kernel = functools.partial(triangle_kernel, tok, blocks)
        if not leaves:
            kernel = lambda *refs: triangle_kernel(tok, blocks, *refs, None, None)
        extra = [pltpu.VMEM(back_shape.shape, BF16), pltpu.SemaphoreType.DMA((blocks,))]
        return call(
            kernel,
            back_shape,
            [
                wide,
                pltpu.VMEM((share, blocks * tok, blocks * LANES // 2), BF16),
                pltpu.VMEM((share, blocks * tok, blocks * LANES // 2), BF16),
                pltpu.VMEM((share, blocks * tok, blocks * LANES // 2), F32),
                thin,
                *(extra if leaves else []),
            ],
            "triangle",
            cost,
            value,
            far_out=(0,) if leaves else (),
        )

    send, sides = call(
        front_kernel,
        (send_shape, shape((width, 2 * tok), BF16)),
        [wide, pltpu.VMEM((n_row, n_col * atom_feats.shape[1], atom_feats.shape[2]), BF16), here, pltpu.SemaphoreType.DMA],
        "front",
        cost,
        bounds,
        same,
        other,
        tokens,
        embedded,
        w_atom,
        w_pair,
        plain,
        chosen,
        mask,
        column(ln_tri[0]),
        side_weights(w_tri_in[0]),
        far=(7,),
        scalar=(0,),
    )
    arrived = exchange(send, COL + ROW)
    arrived, sides, pair_in, d_pair, valid, w_tri_in, w_tri_out, ln_tri, ln_tri_out, w_up, w_down, ln_trans = (
        lax.optimization_barrier(
            (arrived, sides, pair_in, d_pair, valid, w_tri_in, w_tri_out, ln_tri, ln_tri_out, w_up, w_down, ln_trans)
        )
    )
    tri = exchange(triangle(arrived, True), ROW + COL)
    w_gates = w_tri_in[:, :, 4 * inner :].swapaxes(1, 2)
    w_outs = [by_owner(w_tri_out[u], u).T for u in range(2)]
    gains_out = [column(by_owner(ln_tri_out[u], u)) for u in range(2)]
    pair, gate = call(
        first_gate_kernel,
        (flat, flat),
        [strided, here, gates, pltpu.SemaphoreType.DMA((2,))],
        "first_gate",
        cost,
        pair_in[0],
        sides,
        column(ln_tri[0]),
        w_gates[0],
        far_out=(0, 1),
    )
    turned_grad = call(
        turn_kernel,
        shape((count, width), BF16),
        [strided, pltpu.VMEM((count, width), BF16), pltpu.SemaphoreType.DMA],
        "turn",
        cost,
        d_pair[0],
        far_out=(0,),
    )
    late = [gains_out[1], w_outs[1], column(ln_trans), w_up.T, w_down.T, turned_grad]
    ready = [
        gains_out[0],
        w_outs[0],
        valid.T.reshape(groups, span),
        column(ln_tri[1]),
        side_weights(w_tri_in[1]),
        w_gates[1],
    ]
    ready, late = lax.optimization_barrier((ready, late))
    send, pair, gate = call(
        middle_kernel,
        (send_shape, flat, flat),
        [thin, wide, here, gates, pltpu.SemaphoreType.DMA((2, groups))],
        "middle",
        cost,
        tri,
        pair,
        gate,
        *ready,
        far=(1, 2),
    )
    arrived = exchange(send, ROW + COL)
    tri = exchange(triangle(arrived, False), ROW + COL)
    grad, hidden, pair = call(
        last_kernel,
        (shape((expand, width), BF16), shape((groups, expand, span), BF16), flat),
        [
            thin,
            pltpu.VMEM((expand, width), F32),
            pltpu.VMEM((count, width), BF16),
            pltpu.VMEM((groups, expand, span), BF16),
            here,
            pltpu.VMEM((expand, width), BF16),
            pltpu.SemaphoreType.DMA((2,)),
            pltpu.SemaphoreType.DMA((2, groups)),
        ],
        "last",
        2 * cost,
        tri,
        pair,
        gate,
        late[0],
        late[1],
        late[2],
        late[3],
        late[5],
        far=(7,),
        far_out=(0, 1, 2),
    )
    everyone = devices * lax.axis_size("rep")
    grad = exchange(grad.reshape(everyone, expand // everyone, width), ROW + COL + ("rep",))
    result = call(
        down_kernel,
        shape((tok, tok, width), BF16),
        [strided],
        "down",
        cost,
        hidden,
        pair,
        late[4],
    )
    return (result[None], jnp.sum(grad.astype(F32), axis=0))


def solution(mesh):
    rows, cols, reps = (mesh.shape[name] for name in ("row", "col", "rep"))
    parts = Mesh(
        mesh.devices.reshape(rows // 2, 2, cols // 2, 2, reps), ROW + COL + ("rep",)
    )
    pair = P("rep", ROW, COL, None)
    return jax.shard_map(
        local,
        mesh=parts,
        in_specs=(
            P("rep", ROW + COL, None),
            P("rep", ROW + COL),
            P("rep", None),
            P("rep", None),
            pair,
            P("rep", ROW, COL),
            *[P()] * 10,
            pair,
        ),
        out_specs=(pair, P(ROW + COL + ("rep",), None)),
        check_vma=False,
    )
```
